256 devices in a mesh: tensor: 16 (over y_lo, z), draw: 4 (over x), batch: 4 (over y_hi, core).
Axes of the slice: x: 4, y: 4 (y_hi: 2, y_lo: 2; y = y_hi * 2 + y_lo), z: 8, core: 2. Of those that a mesh axis runs over, the one named last changes fastest.
Arguments:
- tokens: bfloat16 [4, 512, 4608], P('draw', None, ('batch', 'tensor')), may hold values from -6 to 6
- cotangent: bfloat16 [4, 512, 4608], P('draw', None, ('batch', 'tensor')), may hold values from -6 to 6
- gate_up_weight: bfloat16 [2, 4608, 18432], P(None, 'batch', ('tensor', 'draw')), may hold values from -0.09375 to 0.09375
- down_weight: bfloat16 [18432, 4608], P(('tensor', 'draw'), 'batch'), may hold values from -0.046875 to 0.046875
- gate_up_noise: bfloat16 [4, 2, 4608, 18432], P('draw', None, 'batch', 'tensor'), may hold values from -1 to 1
- down_noise: bfloat16 [4, 18432, 4608], P('draw', 'tensor', 'batch'), may hold values from -1 to 1
- gate_up_left: bfloat16 [2, 4608, 64], P(None, 'batch'), may hold values from -0.09375 to 0.09375
- gate_up_right: bfloat16 [2, 64, 18432], P(None, None, 'tensor'), may hold values from -0.75 to 0.75
- down_left: bfloat16 [18432, 64], P('tensor'), may hold values from -0.046875 to 0.046875
- down_right: bfloat16 [64, 4608], P(None, 'batch'), may hold values from -0.75 to 0.75
Outputs:
- layer_out: bfloat16 [4, 512, 4608], P('draw', None, ('batch', 'tensor'))
- input_grad: bfloat16 [4, 512, 4608], P('draw', None, ('batch', 'tensor'))
- grad_gate_up_left: bfloat16 [2, 4608, 64], P(None, 'batch')
- grad_gate_up_right: bfloat16 [2, 64, 18432], P(None, None, 'tensor')
- grad_down_left: bfloat16 [18432, 64], P('tensor')
- grad_down_right: bfloat16 [64, 4608], P(None, 'batch')
The draws below stay inside these ranges and needn't reach their ends.
All inputs are finite; a program needn't handle non-finite values.
Results may differ from the reference program's by a relative error of at most 0.029.
Values may be sent and summed in bfloat16 or wider, within the bound.
A program may use at most 128 MiB of HBM per device.

```python
import jax
import jax.numpy as jnp
from jax import lax

D = 4608
FF = 18432
R = 64
TOKENS = 512
NDRAW = 4


def shard_levels(rng, shape, cuts, smallest, high):
    gain, own = 1.0, jax.random.fold_in(rng, 6)
    for dim, parts in cuts:
        heights = jnp.exp(jax.random.uniform(jax.random.fold_in(own, dim), (parts,), jnp.float32, smallest / len(cuts), high / len(cuts)))
        gain = gain * jnp.repeat(heights, shape[dim] // parts).reshape([-1 if axis == dim else 1 for axis in range(len(shape))])
    return gain


def scatter_about(own_key, shape, deviation, most, pieces=(), held_as=jnp.bfloat16):
    values = jax.random.normal(own_key, shape, jnp.float32) * deviation
    if len(pieces) > 0:
        values = shard_levels(own_key, shape, pieces, -0.22, 0.18) * values
    return jnp.clip(values, min=-most, max=most).astype(held_as)


def setup_inputs(seed: int = 0) -> dict:
    splits = jax.random.split(jax.random.key(seed), 11)
    return {
        "tokens": scatter_about(splits[0], (NDRAW, TOKENS, D), 1.0, 6.0, ((0, 4), (2, 64))),
        "cotangent": scatter_about(splits[1], (NDRAW, TOKENS, D), 1.0, 6.0, ((0, 4), (2, 64))),
        "gate_up_weight": scatter_about(splits[2], (2, D, FF), D ** -0.5, 0.09375, ((1, 4), (2, 64))),
        "down_weight": scatter_about(splits[3], (FF, D), FF ** -0.5, 0.046875, ((0, 64), (1, 4))),
        "gate_up_noise": jnp.clip(jax.random.uniform(splits[4], (NDRAW, 2, D, FF), jnp.float32, -1.0, 1.0) * shard_levels(splits[4], (NDRAW, 2, D, FF), ((0, 4), (2, 4), (3, 16)), -0.4, 0.0), -1.0, 1.0).astype(jnp.bfloat16),
        "down_noise": jnp.clip(jax.random.uniform(splits[5], (NDRAW, FF, D), jnp.float32, -1.0, 1.0) * shard_levels(splits[5], (NDRAW, FF, D), ((0, 4), (1, 16), (2, 4)), -0.4, 0.0), -1.0, 1.0).astype(jnp.bfloat16),
        "gate_up_left": scatter_about(splits[6], (2, D, R), D ** -0.5, 0.09375, ((1, 4),)),
        "gate_up_right": scatter_about(splits[7], (2, R, FF), R ** -0.5, 0.75, ((2, 16),)),
        "down_left": scatter_about(splits[8], (FF, R), FF ** -0.5, 0.046875, ((0, 16),)),
        "down_right": scatter_about(splits[9], (R, D), R ** -0.5, 0.75, ((1, 4),)),
    }


noise_sigma = 0.5
root_coeff = 0.7978845608028654
cubic_coeff = 0.044715


def gelu_pair(value):
    inner = root_coeff * (value + cubic_coeff * value * value * value)
    bend = jnp.tanh(inner)
    result = 0.5 * value * (1.0 + bend)
    slope = 0.5 * (1.0 + bend) + 0.5 * value * (1.0 - bend * bend) * root_coeff * (1.0 + 3.0 * cubic_coeff * value * value)
    return result, slope


def perturb(weight, noise):
    return (weight.astype(jnp.float32) * (1.0 + noise_sigma * noise.astype(jnp.float32))).astype(jnp.bfloat16)


def highest(left, right):
    return jnp.dot(left, right, precision=lax.Precision.HIGHEST, preferred_element_type=jnp.float32)


def reference(tokens, cotangent, gate_up_weight, down_weight, gate_up_noise, down_noise, gate_up_left, gate_up_right, down_left, down_right):
    scale_grad = (NDRAW * TOKENS) ** -0.5
    right_gate = gate_up_right.astype(jnp.float32)
    left_gate = gate_up_left.astype(jnp.float32)
    down_left_f = down_left.astype(jnp.float32)
    down_right_f = down_right.astype(jnp.float32)
    acc_left = jnp.zeros((2, D, R), jnp.float32)
    acc_right = jnp.zeros((2, R, FF), jnp.float32)
    acc_down_left = jnp.zeros((FF, R), jnp.float32)
    acc_down_right = jnp.zeros((R, D), jnp.float32)
    outputs = []
    in_grads = []
    for draw in range(NDRAW):
        inputs = tokens[draw]
        cot = cotangent[draw]
        noisy_gu = perturb(gate_up_weight, gate_up_noise[draw])
        noisy_dn = perturb(down_weight, down_noise[draw])
        low_gu = [jnp.dot(inputs, gate_up_left[k], preferred_element_type=jnp.float32) for k in range(2)]
        pre = [jnp.dot(inputs, noisy_gu[k], preferred_element_type=jnp.float32) + highest(low_gu[k], right_gate[k]) for k in range(2)]
        active, slope = gelu_pair(pre[0])
        hidden = (active * pre[1]).astype(jnp.bfloat16)
        low_dn = jnp.dot(hidden, down_left, preferred_element_type=jnp.float32)
        result = jnp.dot(hidden, noisy_dn, preferred_element_type=jnp.float32) + highest(low_dn, down_right_f)
        outputs.append(result.astype(jnp.bfloat16))
        back_low = jnp.dot(cot, down_right.T, preferred_element_type=jnp.float32)
        hidden_grad = jnp.dot(cot, noisy_dn.T, preferred_element_type=jnp.float32) + highest(back_low, down_left_f.T)
        grad_gate = (hidden_grad * pre[1] * slope).astype(jnp.bfloat16)
        grad_up = (hidden_grad * active).astype(jnp.bfloat16)
        pre_grad = [grad_gate, grad_up]
        rank_grad = [jnp.dot(pre_grad[k], gate_up_right[k].T, preferred_element_type=jnp.float32) for k in range(2)]
        total = jnp.zeros((TOKENS, D), jnp.float32)
        for k in range(2):
            total = total + jnp.dot(pre_grad[k], noisy_gu[k].T, preferred_element_type=jnp.float32)
            total = total + highest(rank_grad[k], left_gate[k].T)
        in_grads.append(total.astype(jnp.bfloat16))
        inputs_f = inputs.astype(jnp.float32)
        acc_left = acc_left + jnp.stack([highest(inputs_f.T, rank_grad[k]) for k in range(2)])
        acc_right = acc_right + jnp.stack([highest(low_gu[k].T, pre_grad[k].astype(jnp.float32)) for k in range(2)])
        acc_down_left = acc_down_left + highest(hidden.astype(jnp.float32).T, back_low)
        acc_down_right = acc_down_right + highest(low_dn.T, cot.astype(jnp.float32))
    layer_out = jnp.stack(outputs)
    input_grad = jnp.stack(in_grads)
    return (layer_out, input_grad,
            (scale_grad * acc_left).astype(jnp.bfloat16),
            (scale_grad * acc_right).astype(jnp.bfloat16),
            (scale_grad * acc_down_left).astype(jnp.bfloat16),
            (scale_grad * acc_down_right).astype(jnp.bfloat16))
```

```python
import jax
import jax.numpy as jnp
from jax import lax
from jax.sharding import PartitionSpec as P

noise_sigma = 0.5
root_coeff = 0.7978845608028654
cubic_coeff = 0.044715


def gelu_pair(value):
    inner = root_coeff * (value + cubic_coeff * value * value * value)
    bend = jnp.tanh(inner)
    result = 0.5 * value * (1.0 + bend)
    slope = 0.5 * (1.0 + bend) + 0.5 * value * (1.0 - bend * bend) * root_coeff * (
        1.0 + 3.0 * cubic_coeff * value * value
    )
    return (result, slope)


def perturb(weight, noise):
    return (weight.astype(jnp.float32) * (1.0 + noise_sigma * noise.astype(jnp.float32))).astype(
        jnp.bfloat16
    )


def highest(left, right):
    return jnp.dot(left, right, precision=lax.Precision.HIGHEST, preferred_element_type=jnp.float32)


def on_device(
    tokens,
    cotangent,
    gate_up_weight,
    down_weight,
    gate_up_noise,
    down_noise,
    gate_up_left,
    gate_up_right,
    down_left,
    down_right,
):
    noise_gu = gate_up_noise[0]
    noise_dn = down_noise[0]
    rows_all = lax.all_gather(tokens[0], "tensor", axis=1, tiled=True)
    total_tokens = rows_all.shape[0]
    scale_grad = (lax.axis_size("draw") * total_tokens) ** (-0.5)
    right_gate = gate_up_right.astype(jnp.float32)
    left_gate = gate_up_left.astype(jnp.float32)
    down_left_f = down_left.astype(jnp.float32)
    down_right_f = down_right.astype(jnp.float32)
    noisy_gu = perturb(lax.all_gather(gate_up_weight, "draw", axis=2, tiled=True), noise_gu)
    noisy_dn = perturb(lax.all_gather(down_weight, "draw", axis=0, tiled=True), noise_dn)
    direct_gu = jnp.einsum("td,kdc->ktc", rows_all, noisy_gu, preferred_element_type=jnp.float32)
    low_part = jnp.einsum("td,kdr->ktr", rows_all, gate_up_left, preferred_element_type=jnp.float32)
    pre_part = direct_gu + jnp.einsum(
        "ktr,krc->ktc",
        low_part,
        right_gate,
        precision=lax.Precision.HIGHEST,
        preferred_element_type=jnp.float32,
    )
    pre = lax.psum_scatter(
        pre_part.astype(jnp.bfloat16), "batch", scatter_dimension=1, tiled=True
    ).astype(jnp.float32)
    active, slope = gelu_pair(pre[0])
    hidden = (active * pre[1]).astype(jnp.bfloat16)
    hidden_all = lax.all_gather(hidden, "batch", axis=0, tiled=True)
    low_down_part = jnp.dot(hidden_all, down_left, preferred_element_type=jnp.float32)
    direct_dn = jnp.dot(hidden_all, noisy_dn, preferred_element_type=jnp.float32)
    out_part = direct_dn + highest(low_down_part, down_right_f)
    cot_all = lax.all_gather(cotangent[0], "tensor", axis=1, tiled=True)
    back_low_part = jnp.einsum("td,rd->tr", cot_all, down_right, preferred_element_type=jnp.float32)
    direct_hid = jnp.einsum("td,cd->tc", cot_all, noisy_dn, preferred_element_type=jnp.float32)
    hid_part = direct_hid + highest(back_low_part, down_left_f.T)
    hidden_grad = lax.psum_scatter(
        hid_part.astype(jnp.bfloat16), "batch", scatter_dimension=0, tiled=True
    ).astype(jnp.float32)
    grad_gate = (hidden_grad * pre[1] * slope).astype(jnp.bfloat16)
    grad_up = (hidden_grad * active).astype(jnp.bfloat16)
    pre_grad = jnp.stack([grad_gate, grad_up])
    pre_grad_all = lax.all_gather(pre_grad, "batch", axis=1, tiled=True)
    rank_part = jnp.einsum(
        "ktc,krc->ktr", pre_grad_all, gate_up_right, preferred_element_type=jnp.float32
    )
    direct_in = jnp.einsum(
        "ktc,kdc->td", pre_grad_all, noisy_gu, preferred_element_type=jnp.float32
    )
    in_part = direct_in + jnp.einsum(
        "ktr,kdr->td",
        rank_part,
        left_gate,
        precision=lax.Precision.HIGHEST,
        preferred_element_type=jnp.float32,
    )
    rows_f = rows_all.astype(jnp.float32)
    left_term = jnp.einsum(
        "ktr,td->krd",
        rank_part,
        rows_f,
        precision=lax.Precision.HIGHEST,
        preferred_element_type=jnp.float32,
    )
    down_right_term = highest(low_down_part.T, cot_all.astype(jnp.float32))
    right_term = jnp.einsum(
        "ktr,ktc->krc",
        low_part,
        pre_grad_all.astype(jnp.float32),
        precision=lax.Precision.HIGHEST,
        preferred_element_type=jnp.float32,
    )
    down_left_term = highest(back_low_part.T, hidden_all.astype(jnp.float32))
    rank = right_term.shape[1]
    width = out_part.shape[1]
    by_feature = jnp.concatenate(
        [out_part, in_part, left_term.reshape(2 * rank, width), down_right_term]
    ).astype(jnp.bfloat16)
    mine = lax.psum_scatter(by_feature.T, "tensor", scatter_dimension=0, tiled=True)
    layer_out = mine[:, :total_tokens].T
    input_grad = mine[:, total_tokens : 2 * total_tokens].T
    feature_sums = lax.psum(mine[:, 2 * total_tokens :], "draw")
    feature_sums = lax.all_gather(
        (scale_grad * feature_sums.astype(jnp.float32)).astype(jnp.bfloat16),
        "tensor",
        axis=0,
        tiled=True,
    ).T
    by_hidden = jnp.concatenate([right_term.reshape(2 * rank, -1), down_left_term])
    by_hidden = lax.psum_scatter(
        by_hidden.astype(jnp.bfloat16).T, ("draw", "batch"), scatter_dimension=0, tiled=True
    )
    hidden_sums = lax.all_gather(
        (scale_grad * by_hidden.astype(jnp.float32)).astype(jnp.bfloat16),
        ("draw", "batch"),
        axis=0,
        tiled=True,
    ).T
    return (
        layer_out[None],
        input_grad[None],
        jnp.swapaxes(feature_sums[: 2 * rank].reshape(2, rank, width), 1, 2),
        hidden_sums[: 2 * rank].reshape(2, rank, -1),
        hidden_sums[2 * rank :].T,
        feature_sums[2 * rank :],
    )


def solution(mesh):
    in_specs = (
        P("draw", None, ("batch", "tensor")),
        P("draw", None, ("batch", "tensor")),
        P(None, "batch", ("tensor", "draw")),
        P(("tensor", "draw"), "batch"),
        P("draw", None, "batch", "tensor"),
        P("draw", "tensor", "batch"),
        P(None, "batch", None),
        P(None, None, "tensor"),
        P("tensor", None),
        P(None, "batch"),
    )
    out_specs = (
        P("draw", None, ("batch", "tensor")),
        P("draw", None, ("batch", "tensor")),
        P(None, "batch", None),
        P(None, None, "tensor"),
        P("tensor", None),
        P(None, "batch"),
    )
    return jax.shard_map(
        on_device, mesh=mesh, in_specs=in_specs, out_specs=out_specs, check_vma=False
    )
```

```python
import functools

import jax
import jax.numpy as jnp
from jax import lax
from jax.experimental import pallas as pl
from jax.experimental.pallas import tpu as pltpu
from jax.sharding import PartitionSpec as P

MESH = pl.DeviceIdType.MESH
f32, bf16 = jnp.float32, jnp.bfloat16

noise_sigma = 0.5
root_coeff = 0.7978845608028654
cubic_coeff = 0.044715

FEAT, HID, TOK, RANK = 1152, 1152, 512, 64
NX, NZ, NT = 4, 8, 16
SHARD = HID // NX
HALF = SHARD // 2
OWN = FEAT // NT
LANES = TOK // 4
WIDE = TOK + 2 * RANK
MESSAGES = 112


def gelu_pair(value):
    inner = root_coeff * (value + cubic_coeff * value * value * value)
    bend = jnp.tanh(inner)
    result = 0.5 * value * (1.0 + bend)
    slope = 0.5 * (1.0 + bend) + 0.5 * value * (1.0 - bend * bend) * root_coeff * (
        1.0 + 3.0 * cubic_coeff * value * value
    )
    return (result, slope)


def dot(left, right):
    return jnp.dot(left, right, preferred_element_type=f32)


def dot_nt(left, right):
    return lax.dot_general(left, right, (((1,), (1,)), ((), ())), preferred_element_type=f32)


def kernel(
    scale_grad,
    tokcot_in,
    wgu_in,
    wdn_in,
    ngu_in,
    ndn_in,
    left_t,
    right_n,
    down_left_t,
    down_right_n,
    out_ref,
    feature_ref,
    hidden_ref,
    weights,
    noisy,
    noisy_t,
    gathered,
    acts,
    left_c,
    right_c,
    lows,
    ranks,
    part,
    core_in,
    y_out,
    y_in,
    back,
    pieces,
    up_in,
    down_in,
    cross_in,
    draw_in,
    adapters,
    tall,
    hid_part,
    hid_core,
    hid_y_out,
    hid_y_in,
    hid_draw,
    hid_all,
    send_sem,
    recv_sem,
    local_sem,
):
    tensor = lax.axis_index("tensor")
    x = lax.axis_index("draw")
    batch = lax.axis_index("batch")
    yl, z = tensor // NZ, tensor % NZ
    yh, core = batch // 2, batch % 2

    def ring(value, count):
        return (value + count) % count

    x_peers = [{"draw": ring(x + o, NX)} for o in (1, 2, 3)]
    x_right, x_left = x_peers[0], x_peers[2]
    z_up = {"tensor": yl * NZ + ring(z + 1, NZ)}
    z_down = {"tensor": yl * NZ + ring(z - 1, NZ)}
    y_lo = {"tensor": (1 - yl) * NZ + z}
    to_core = {"batch": yh * 2 + 1 - core}
    y_hi = {"batch": (1 - yh) * 2 + core}

    count = [0]
    started = []

    def send(src, dst, where):
        at = count[0]
        count[0] += 1
        assert at < MESSAGES
        copy = pltpu.make_async_remote_copy(
            src_ref=src,
            dst_ref=dst,
            send_sem=send_sem.at[at],
            recv_sem=recv_sem.at[at],
            device_id=where,
            device_id_type=MESH,
        )
        copy.start()
        started.append(copy)
        return copy

    barrier = pltpu.get_barrier_semaphore()
    partners = [*x_peers, z_up, z_down, y_lo, to_core, y_hi]
    for where in partners:
        pl.semaphore_signal(barrier, inc=1, device_id=where, device_id_type=MESH)
    pl.semaphore_wait(barrier, len(partners))

    def rows(owner, first=0, size=SHARD):
        return pl.ds(pl.multiple_of(owner * SHARD + first, 16), size)

    own_copy = pltpu.make_async_copy(tokcot_in, gathered.at[tensor], local_sem.at[0])
    own_copy.start()
    y_copy = send(tokcot_in, gathered.at[tensor], y_lo)
    to_right = [send(wgu_in.at[k], weights.at[k, rows(x)], x_right) for k in (0, 1)]
    to_left = [send(wgu_in.at[k], weights.at[k, rows(x)], x_left) for k in (0, 1)]
    to_right.append(send(wdn_in, weights.at[2, rows(x)], x_right))
    to_left.append(send(wdn_in, weights.at[2, rows(x)], x_left))
    locals_ = [
        pltpu.make_async_copy(ngu_in.at[0], noisy_t.at[0], local_sem.at[1]),
        pltpu.make_async_copy(ngu_in.at[1], noisy_t.at[1], local_sem.at[2]),
        pltpu.make_async_copy(ndn_in, noisy.at[2], local_sem.at[3]),
        pltpu.make_async_copy(wgu_in.at[0], weights.at[0, rows(x)], local_sem.at[4]),
        pltpu.make_async_copy(wgu_in.at[1], weights.at[1, rows(x)], local_sem.at[5]),
        pltpu.make_async_copy(wdn_in, weights.at[2, rows(x)], local_sem.at[6]),
    ]
    for copy in locals_:
        copy.start()

    def gather_rings(ref):
        def hop(step, half, up):
            at = half * NZ + (ring(z - step, NZ) if up else ring(z + step, NZ))
            return send(ref.at[at], ref.at[at], z_up if up else z_down)

        flight = {}
        for half in (0, 1):
            for up in (True, False):
                flight[half, up] = hop(0, half, up)
        for step in (1, 2, 3, 4):
            for half in (0, 1):
                for up in (True, False):
                    last = 4 if (half == 0) == up else 3
                    if step > last:
                        continue
                    flight[half, up].wait_recv()
                    if step < last:
                        flight[half, up] = hop(step, half, up)
            yield step

    def flip(source, target, first, last):
        def body(strip, _):
            k, at = strip // 9, pl.ds(pl.multiple_of((strip % 9) * 128, 128), 128)
            target[k, :, at] = source[k, at, :].T
            return 0

        lax.fori_loop(first, last, body, 0)

    for k in (0, 1):
        left_c[k] = left_t[k].T
        right_c[k] = right_n[k].T
    left_c[2] = down_right_n[...].T
    right_c[2] = down_left_t[...].T
    own_copy.wait()
    y_copy.wait_recv()
    rings = gather_rings(gathered)
    locals_[0].wait()
    locals_[1].wait()
    flip(noisy_t, noisy, 0, 5)
    next(rings)
    flip(noisy_t, noisy, 5, 10)
    next(rings)
    flip(noisy_t, noisy, 10, 15)
    next(rings)
    flip(noisy_t, noisy, 15, 18)
    next(rings)

    def unpack(m, _):
        first, second = gathered[2 * m].astype(f32), gathered[2 * m + 1].astype(f32)
        at = pl.ds(pl.multiple_of(m * 2 * OWN, 16), 2 * OWN)
        acts[0, at, :] = jnp.concatenate([first[:OWN], second[:OWN]]).astype(bf16)
        acts[1, at, :] = jnp.concatenate([first[OWN:], second[OWN:]]).astype(bf16)
        return 0

    lax.fori_loop(0, NZ, unpack, 0)
    lows[0] = dot(left_t[0], acts[0]).astype(bf16)
    lows[1] = dot(left_t[1], acts[0]).astype(bf16)
    lows[2] = dot(down_right_n[...], acts[1]).astype(bf16)
    for copy in locals_[2:]:
        copy.wait()

    x_l, x_r, x_o = ring(x - 1, NX), ring(x + 1, NX), ring(x + 2, NX)
    fwd_right, fwd_left = [], []

    def forward(k):
        to_right[k].wait_recv()
        at = weights.at[k, rows(x_l, 0, HALF)]
        fwd_right.append(send(at, at, x_right))
        to_left[k].wait_recv()
        at = weights.at[k, rows(x_r, HALF, HALF)]
        fwd_left.append(send(at, at, x_left))

    def spread(j, owner):
        def body(k, _):
            at = rows(owner)
            noisy[k, at, :] = (
                weights[k, at, :].astype(f32) * (1.0 + noise_sigma * noisy[k, at, :].astype(f32))
            ).astype(bf16)
            total = dot(noisy[k, at, :], acts[k // 2]) + dot(right_c[k, at, :], lows[k])
            for b in range(4):
                part[j, b % 2, b // 2, k] = total[:, b * LANES : (b + 1) * LANES].astype(bf16)
            return 0

        lax.fori_loop(0, 3, body, 0)
        return send(part.at[j, 1 - core], core_in.at[j], to_core)

    def cores(j, copy):
        copy.wait_recv()
        y_out[j] = (
            part[j, core, 1 - yh].astype(f32) + core_in[j, 1 - yh].astype(f32)
        ).astype(bf16)
        return send(y_out.at[j], y_in.at[j], y_hi)

    def bend(j, owner, copy):
        copy.wait_recv()
        at = rows(owner)

        def whole(k):
            return (
                part[j, core, yh, k].astype(f32)
                + core_in[j, yh, k].astype(f32)
                + y_in[j, k].astype(f32)
            )

        gate, up, grad = whole(0), whole(1), whole(2)
        active, slope = gelu_pair(gate)
        back[batch, 0, at, :] = (grad * up * slope).astype(bf16)
        back[batch, 1, at, :] = (grad * active).astype(bf16)
        back[batch, 2, at, :] = (active * up).astype(bf16)
        mine = back.at[batch, :, at]
        return [send(mine, mine, y_hi), send(mine, mine, to_core)]

    def share(owner, copies):
        copies[0].wait_recv()
        far = back.at[(1 - yh) * 2 + core, :, rows(owner)]
        copies.append(send(far, far, to_core))

    def finish(copies):
        copies[1].wait_recv()
        copies[2].wait_recv()

    forward(0)
    c0 = spread(0, x)
    forward(1)
    c0 = cores(0, c0)
    forward(2)
    c1 = spread(1, x_l)
    c0 = bend(0, x, c0)
    c1 = cores(1, c1)
    c2 = spread(2, x_r)
    share(x, c0)
    c1 = bend(1, x_l, c1)
    c2 = cores(2, c2)
    finish(c0)
    share(x_l, c1)
    c2 = bend(2, x_r, c2)
    finish(c1)
    share(x_r, c2)
    finish(c2)
    for k in range(3):
        fwd_right[k].wait_recv()
        fwd_left[k].wait_recv()
    c3 = spread(3, x_o)
    flip(noisy, noisy_t, 0, 9)
    c3 = cores(3, c3)
    flip(noisy, noisy_t, 9, 18)
    c3 = bend(3, x_o, c3)
    flip(noisy, noisy_t, 18, 27)
    share(x_o, c3)
    finish(c3)

    def all_tokens(k):
        return jnp.concatenate([back[b, k] for b in range(4)], axis=1)

    for k in range(3):
        values = all_tokens(k)
        sheet = right_n[k] if k < 2 else down_left_t[...]
        ranks[pl.ds(k * RANK, RANK), :] = dot(sheet, values).astype(bf16)
        hid_part[pl.ds(k * RANK, RANK), :] = dot_nt(lows[k], values).astype(bf16)

    h1 = send(
        hid_part.at[pl.ds(pl.multiple_of((1 - core) * 96, 16), 96)], hid_core, to_core
    )

    def outputs(m, _):
        at = pl.ds(pl.multiple_of(m * SHARD, 16), SHARD)
        out = dot(noisy_t[2, at, :], all_tokens(2)) + dot(left_c[2, at, :], ranks[128:192, :])
        grad = dot(noisy_t[0, at, :], all_tokens(0)) + dot(left_c[0, at, :], ranks[0:64, :])
        grad = grad + dot(noisy_t[1, at, :], all_tokens(1)) + dot(left_c[1, at, :], ranks[64:128, :])
        right_side = dot_nt(acts[1, at, :], ranks[64:192, :])
        left_side = dot_nt(acts[0, at, :], ranks[0:128, :])
        for i in range(4):
            cut = slice(i * OWN, (i + 1) * OWN)
            pieces[4 * m + i, :, :TOK] = jnp.concatenate([out[cut], grad[cut]]).astype(bf16)
            pieces[4 * m + i, :, TOK:] = jnp.concatenate(
                [right_side[cut], left_side[cut]]
            ).astype(bf16)
        return 0

    lax.fori_loop(0, 4, outputs, 0)

    def pass_on(step, half, up, copy):
        target = half * NZ + (ring(z + 4 - step, NZ) if up else ring(z - 4 + step, NZ))
        box = (up_in if up else down_in).at[step, half]
        if copy is not None:
            copy.wait_recv()
            came = (up_in if up else down_in)[step - 1, half]
            pieces[target] = (pieces[target].astype(f32) + came.astype(f32)).astype(bf16)
        return send(pieces.at[target], box, z_up if up else z_down)

    flight = {}
    flight[0, True] = pass_on(0, 0, True, None)
    flight[1, False] = pass_on(0, 1, False, None)
    flight[1, True] = pass_on(1, 1, True, None)
    flight[0, False] = pass_on(1, 0, False, None)

    h1.wait_recv()
    own_rows = pl.ds(pl.multiple_of(core * 96 + yh * 48, 16), 48)
    far_rows = pl.ds(pl.multiple_of(core * 96 + (1 - yh) * 48, 16), 48)
    own_half = pl.ds(pl.multiple_of(yh * 48, 16), 48)
    far_half = pl.ds(pl.multiple_of((1 - yh) * 48, 16), 48)
    hid_y_out[...] = (
        hid_part[far_rows, :].astype(f32) + hid_core[far_half, :].astype(f32)
    ).astype(bf16)
    h2 = send(hid_y_out, hid_y_in, y_hi)

    flight[0, True] = pass_on(1, 0, True, flight[0, True])
    flight[1, False] = pass_on(1, 1, False, flight[1, False])

    h2.wait_recv()
    hid_draw[x] = (
        hid_part[own_rows, :].astype(f32)
        + hid_core[own_half, :].astype(f32)
        + hid_y_in[...].astype(f32)
    ).astype(bf16)
    h3 = [send(hid_draw.at[x], hid_draw.at[x], where) for where in x_peers]

    flight[1, True] = pass_on(2, 1, True, flight[1, True])
    flight[0, False] = pass_on(2, 0, False, flight[0, False])
    flight[0, True] = pass_on(2, 0, True, flight[0, True])
    flight[1, False] = pass_on(2, 1, False, flight[1, False])

    for copy in h3:
        copy.wait_recv()
    total = (hid_draw[0].astype(f32) + hid_draw[1].astype(f32)) + (
        hid_draw[2].astype(f32) + hid_draw[3].astype(f32)
    )
    hid_all[own_rows, :] = (scale_grad * total).astype(bf16)
    h4 = [
        send(hid_all.at[own_rows], hid_all.at[own_rows], y_hi),
        send(hid_all.at[own_rows], hid_all.at[own_rows], to_core),
    ]

    flight[1, True] = pass_on(3, 1, True, flight[1, True])
    flight[0, False] = pass_on(3, 0, False, flight[0, False])
    flight[0, True] = pass_on(3, 0, True, flight[0, True])
    flight[1, False] = pass_on(3, 1, False, flight[1, False])

    h4[0].wait_recv()
    h4.append(send(hid_all.at[far_rows], hid_all.at[far_rows], to_core))

    for copy in flight.values():
        copy.wait_recv()

    def over_z(half):
        return (
            pieces[half * NZ + z].astype(f32)
            + up_in[3, half].astype(f32)
            + down_in[3, half].astype(f32)
        )

    y_piece = (1 - yl) * NZ + z
    pieces[y_piece] = over_z(1 - yl).astype(bf16)
    cross = send(pieces.at[y_piece], cross_in, y_lo)
    mine = over_z(yl)
    h4[1].wait_recv()
    h4[2].wait_recv()
    hidden_ref[...] = hid_all[...]
    cross.wait_recv()
    mine = mine + cross_in[...].astype(f32)
    draw_in[x] = mine[:, TOK:].astype(bf16)
    d1 = [send(draw_in.at[x], draw_in.at[x], where) for where in x_peers]
    out_ref[...] = mine[:, :TOK].astype(bf16)
    for copy in d1:
        copy.wait_recv()
    total = (draw_in[0].astype(f32) + draw_in[1].astype(f32)) + (
        draw_in[2].astype(f32) + draw_in[3].astype(f32)
    )
    adapters[tensor] = (scale_grad * total).astype(bf16)
    y_copy = send(adapters.at[tensor], adapters.at[tensor], y_lo)
    y_copy.wait_recv()
    for _ in gather_rings(adapters):
        pass
    for t in range(NT):
        both = adapters[t].astype(f32)
        tall[1, t * OWN : (t + 1) * OWN, :] = both[:OWN]
        tall[0, t * OWN : (t + 1) * OWN, :] = both[OWN:]
    feature_ref[: 2 * RANK, :] = tall[0].T.astype(bf16)
    feature_ref[2 * RANK :, :] = tall[1].T[RANK:].astype(bf16)
    for copy in started:
        copy.wait_send()


def on_device(
    tokens,
    cotangent,
    gate_up_weight,
    down_weight,
    gate_up_noise,
    down_noise,
    gate_up_left,
    gate_up_right,
    down_left,
    down_right,
):
    scale_grad = (NX * TOK) ** (-0.5)
    vmem, anywhere = pl.BlockSpec(memory_space=pltpu.VMEM), pl.BlockSpec(memory_space=pl.ANY)
    tokcot = jnp.concatenate([tokens[0].T, cotangent[0].T])
    scratch = [
        pltpu.VMEM((3, HID, FEAT), bf16),
        pltpu.VMEM((3, HID, FEAT), bf16),
        pltpu.VMEM((3, FEAT, HID), bf16),
        pltpu.VMEM((NT, 2 * OWN, TOK), bf16),
        pltpu.VMEM((2, FEAT, TOK), bf16),
        pltpu.VMEM((3, FEAT, RANK), bf16),
        pltpu.VMEM((3, HID, RANK), bf16),
        pltpu.VMEM((3, RANK, TOK), bf16),
        pltpu.VMEM((3 * RANK, TOK), bf16),
        pltpu.VMEM((NX, 2, 2, 3, SHARD, LANES), bf16),
        pltpu.VMEM((NX, 2, 3, SHARD, LANES), bf16),
        pltpu.VMEM((NX, 3, SHARD, LANES), bf16),
        pltpu.VMEM((NX, 3, SHARD, LANES), bf16),
        pltpu.VMEM((4, 3, HID, LANES), bf16),
        pltpu.VMEM((NT, 2 * OWN, WIDE), bf16),
        pltpu.VMEM((4, 2, 2 * OWN, WIDE), bf16),
        pltpu.VMEM((4, 2, 2 * OWN, WIDE), bf16),
        pltpu.VMEM((2 * OWN, WIDE), bf16),
        pltpu.VMEM((NX, 2 * OWN, 2 * RANK), bf16),
        pltpu.VMEM((NT, 2 * OWN, 2 * RANK), bf16),
        pltpu.VMEM((2, FEAT, 2 * RANK), f32),
        pltpu.VMEM((3 * RANK, HID), bf16),
        pltpu.VMEM((96, HID), bf16),
        pltpu.VMEM((48, HID), bf16),
        pltpu.VMEM((48, HID), bf16),
        pltpu.VMEM((NX, 48, HID), bf16),
        pltpu.VMEM((3 * RANK, HID), bf16),
        pltpu.SemaphoreType.DMA((MESSAGES,)),
        pltpu.SemaphoreType.DMA((MESSAGES,)),
        pltpu.SemaphoreType.DMA((8,)),
    ]
    both, feature, hidden = pl.pallas_call(
        functools.partial(kernel, scale_grad),
        out_shape=(
            jax.ShapeDtypeStruct((2 * OWN, TOK), bf16),
            jax.ShapeDtypeStruct((3 * RANK, FEAT), bf16),
            jax.ShapeDtypeStruct((3 * RANK, HID), bf16),
        ),
        in_specs=[anywhere] * 5 + [vmem] * 4,
        out_specs=(vmem, vmem, vmem),
        scratch_shapes=scratch,
        compiler_params=pltpu.CompilerParams(
            collective_id=0, has_side_effects=True, vmem_limit_bytes=60 * 2**20
        ),
    )(
        tokcot,
        jnp.swapaxes(gate_up_weight, 1, 2),
        down_weight,
        gate_up_noise[0],
        down_noise[0],
        jnp.swapaxes(gate_up_left, 1, 2),
        gate_up_right,
        down_left.T,
        down_right,
    )
    return (
        both[:OWN].T[None],
        both[OWN:].T[None],
        jnp.swapaxes(feature[: 2 * RANK].reshape(2, RANK, FEAT), 1, 2),
        hidden[: 2 * RANK].reshape(2, RANK, HID),
        hidden[2 * RANK :].T,
        feature[2 * RANK :],
    )


def solution(mesh):
    in_specs = (
        P("draw", None, ("batch", "tensor")),
        P("draw", None, ("batch", "tensor")),
        P(None, "batch", ("tensor", "draw")),
        P(("tensor", "draw"), "batch"),
        P("draw", None, "batch", "tensor"),
        P("draw", "tensor", "batch"),
        P(None, "batch", None),
        P(None, None, "tensor"),
        P("tensor", None),
        P(None, "batch"),
    )
    out_specs = (
        P("draw", None, ("batch", "tensor")),
        P("draw", None, ("batch", "tensor")),
        P(None, "batch", None),
        P(None, None, "tensor"),
        P("tensor", None),
        P(None, "batch"),
    )
    return jax.shard_map(
        on_device, mesh=mesh, in_specs=in_specs, out_specs=out_specs, check_vma=False
    )
```

```python
import functools

import jax
import jax.numpy as jnp
from jax import lax
from jax.experimental import pallas as pl
from jax.experimental.pallas import tpu as pltpu
from jax.sharding import PartitionSpec as P

MESH = pl.DeviceIdType.MESH
f32, bf16 = jnp.float32, jnp.bfloat16

noise_sigma = 0.5
root_coeff = 0.7978845608028654
cubic_coeff = 0.044715

FEAT, HID, TOK, RANK = 1152, 1152, 512, 64
NX, NZ, NT = 4, 8, 16
SHARD = HID // NX
HALF = SHARD // 2
OWN = FEAT // NT
PACK = OWN + 40
LANES = TOK // 4
EARLY = 768
MESSAGES = 128


def gelu_pair(value):
    inner = root_coeff * (value + cubic_coeff * value * value * value)
    bend = jnp.tanh(inner)
    result = 0.5 * value * (1.0 + bend)
    slope = 0.5 * (1.0 + bend) + 0.5 * value * (1.0 - bend * bend) * root_coeff * (
        1.0 + 3.0 * cubic_coeff * value * value
    )
    return (result, slope)


def dot(left, right):
    return jnp.dot(left, right, preferred_element_type=f32)


def dot_nt(left, right):
    return lax.dot_general(left, right, (((1,), (1,)), ((), ())), preferred_element_type=f32)


def kernel(
    scale_grad,
    tokens_in,
    cotangent_in,
    wgu_in,
    wdn_in,
    ngu_in,
    ndn_in,
    left_t,
    right_n,
    down_left_t,
    down_right_n,
    out_ref,
    grad_ref,
    left_ref,
    right_ref,
    down_left_ref,
    down_right_ref,
    weights,
    noisy,
    noisy_t,
    gathered,
    acts,
    left_c,
    right_c,
    right_a,
    lows,
    ranks,
    part,
    core_in,
    y_out,
    y_in,
    back,
    early_out,
    early_grad,
    pieces,
    up_in,
    down_in,
    cross_in,
    rank_out,
    rank_in,
    rank_all,
    draw_in,
    adapters,
    tall,
    hid_part,
    hid_core,
    hid_y_out,
    hid_y_in,
    hid_draw,
    hid_all,
    send_sem,
    recv_sem,
    local_sem,
):
    tensor = lax.axis_index("tensor")
    x = lax.axis_index("draw")
    batch = lax.axis_index("batch")
    yl, z = tensor // NZ, tensor % NZ
    yh, core = batch // 2, batch % 2

    def ring(value, count):
        return (value + count) % count

    x_peers = [{"draw": ring(x + o, NX)} for o in (1, 2, 3)]
    x_right, x_left = x_peers[0], x_peers[2]
    z_up = {"tensor": yl * NZ + ring(z + 1, NZ)}
    z_down = {"tensor": yl * NZ + ring(z - 1, NZ)}
    y_lo = {"tensor": (1 - yl) * NZ + z}
    to_core = {"batch": yh * 2 + 1 - core}
    y_hi = {"batch": (1 - yh) * 2 + core}

    count = [0]
    started = []

    def send(src, dst, where):
        at = count[0]
        count[0] += 1
        assert at < MESSAGES
        copy = pltpu.make_async_remote_copy(
            src_ref=src,
            dst_ref=dst,
            send_sem=send_sem.at[at],
            recv_sem=recv_sem.at[at],
            device_id=where,
            device_id_type=MESH,
        )
        copy.start()
        started.append(copy)
        return copy

    gathered[tensor] = jnp.concatenate(
        [tokens_in[...].astype(f32), cotangent_in[...].astype(f32)]
    ).astype(bf16)

    barrier = pltpu.get_barrier_semaphore()
    tensor_peers = [(tensor + o) % NT for o in range(1, NT)]
    partners = [*x_peers, to_core, y_hi, *({"tensor": peer} for peer in tensor_peers)]
    for where in partners:
        pl.semaphore_signal(barrier, inc=1, device_id=where, device_id_type=MESH)
    pl.semaphore_wait(barrier, len(partners))

    def rows(owner, first=0, size=SHARD):
        return pl.ds(pl.multiple_of(owner * SHARD + first, 16), size)

    owners = [x, ring(x - 1, NX), ring(x + 1, NX), ring(x + 2, NX)]

    def place(owner):
        away = ring(owner - x, NX)
        turn = (2 * away + 3 * (away // 2)) % 4
        return pl.ds(pl.multiple_of(turn * SHARD, 16), SHARD)

    def block(j):
        return pl.ds(j * SHARD, SHARD)

    y_copy = send(gathered.at[tensor], gathered.at[tensor], y_lo)
    to_right = [send(wgu_in.at[k], weights.at[k, rows(x)], x_right) for k in (0, 1)]
    to_left = [send(wgu_in.at[k], weights.at[k, rows(x)], x_left) for k in (0, 1)]
    to_right.append(send(wdn_in, weights.at[2, rows(x)], x_right))
    to_left.append(send(wdn_in, weights.at[2, rows(x)], x_left))
    locals_ = [
        pltpu.make_async_copy(ngu_in.at[0], noisy_t.at[0], local_sem.at[1]),
        pltpu.make_async_copy(ngu_in.at[1], noisy_t.at[1], local_sem.at[2]),
        pltpu.make_async_copy(wgu_in.at[0], weights.at[0, rows(x)], local_sem.at[3]),
        pltpu.make_async_copy(wgu_in.at[1], weights.at[1, rows(x)], local_sem.at[4]),
        pltpu.make_async_copy(wdn_in, weights.at[2, rows(x)], local_sem.at[5]),
    ]
    locals_ += [
        pltpu.make_async_copy(
            ndn_in.at[rows(owners[j])], noisy.at[2, block(j)], local_sem.at[6 + j]
        )
        for j in range(NX)
    ]
    for copy in locals_:
        copy.start()

    def gather_rings(ref):
        def hop(step, half, up):
            at = half * NZ + (ring(z - step, NZ) if up else ring(z + step, NZ))
            return send(ref.at[at], ref.at[at], z_up if up else z_down)

        flight = {}
        for half in (0, 1):
            for up in (True, False):
                flight[half, up] = hop(0, half, up)
        for step in (1, 2, 3, 4):
            for half in (0, 1):
                for up in (True, False):
                    last = 4 if (half == 0) == up else 3
                    if step > last:
                        continue
                    flight[half, up].wait_recv()
                    if step < last:
                        flight[half, up] = hop(step, half, up)
            yield step

    def flip_noise(first, last):
        def body(strip, _):
            k, at = strip // 9, pl.ds(pl.multiple_of((strip % 9) * 128, 128), 128)
            turned = noisy_t[k, at, :].T
            for i in range(NX):
                noisy[k, place(i), at] = turned[i * SHARD : (i + 1) * SHARD]
            return 0

        lax.fori_loop(first, last, body, 0)

    def flip_back(first, last):
        def body(strip, _):
            k, at = strip // (last - first), pl.ds(
                pl.multiple_of((first + strip % (last - first)) * 128, 128), 128
            )
            noisy_t[k, :, at] = noisy[k, at, :].T
            return 0

        lax.fori_loop(0, 3 * (last - first), body, 0)

    for k in range(3):
        left_c[k] = (left_t[k] if k < 2 else down_right_n[...]).T
        turned = (right_n[k] if k < 2 else down_left_t[...]).T
        for i in range(NX):
            right_c[k, place(i), :] = turned[i * SHARD : (i + 1) * SHARD]
        right_a[k] = right_c[k].T
    y_copy.wait_recv()
    rings = gather_rings(gathered)
    locals_[0].wait()
    locals_[1].wait()
    flip_noise(0, 5)
    next(rings)
    flip_noise(5, 10)
    next(rings)
    flip_noise(10, 15)
    next(rings)
    flip_noise(15, 18)
    next(rings)

    def unpack(m, _):
        first, second = gathered[2 * m].astype(f32), gathered[2 * m + 1].astype(f32)
        at = pl.ds(pl.multiple_of(m * 2 * OWN, 16), 2 * OWN)
        acts[0, at, :] = jnp.concatenate([first[:OWN], second[:OWN]]).astype(bf16)
        acts[1, at, :] = jnp.concatenate([first[OWN:], second[OWN:]]).astype(bf16)
        return 0

    lax.fori_loop(0, NZ, unpack, 0)
    lows[0] = dot(left_t[0], acts[0]).astype(bf16)
    lows[1] = dot(left_t[1], acts[0]).astype(bf16)
    lows[2] = dot(down_right_n[...], acts[1]).astype(bf16)
    for copy in locals_[2:]:
        copy.wait()

    x_l, x_r = owners[1], owners[2]
    fwd_right, fwd_left = [], []

    def forward(k):
        to_right[k].wait_recv()
        at = weights.at[k, rows(x_l, 0, HALF)]
        fwd_right.append(send(at, at, x_right))
        to_left[k].wait_recv()
        at = weights.at[k, rows(x_r, HALF, HALF)]
        fwd_left.append(send(at, at, x_left))

    def spread(j):
        def body(k, _):
            noisy[k, block(j), :] = (
                weights[k, rows(owners[j]), :].astype(f32)
                * (1.0 + noise_sigma * noisy[k, block(j), :].astype(f32))
            ).astype(bf16)
            total = dot(noisy[k, block(j), :], acts[k // 2])
            total = total + dot(right_c[k, block(j), :], lows[k])
            for b in range(4):
                part[j, b % 2, b // 2, k] = total[:, b * LANES : (b + 1) * LANES].astype(bf16)
            return 0

        lax.fori_loop(0, 3, body, 0)
        return send(part.at[j, 1 - core], core_in.at[j], to_core)

    def cores(j, copy):
        copy.wait_recv()
        y_out[j] = (
            part[j, core, 1 - yh].astype(f32) + core_in[j, 1 - yh].astype(f32)
        ).astype(bf16)
        return send(y_out.at[j], y_in.at[j], y_hi)

    def bend(j, copy):
        copy.wait_recv()
        at = block(j)

        def whole(k):
            return (
                part[j, core, yh, k].astype(f32)
                + core_in[j, yh, k].astype(f32)
                + y_in[j, k].astype(f32)
            )

        gate, up, grad = whole(0), whole(1), whole(2)
        active, slope = gelu_pair(gate)
        back[batch, 0, at, :] = (grad * up * slope).astype(bf16)
        back[batch, 1, at, :] = (grad * active).astype(bf16)
        back[batch, 2, at, :] = (active * up).astype(bf16)
        mine = back.at[batch, :, at]
        return [send(mine, mine, y_hi), send(mine, mine, to_core)]

    def share(j, copies):
        copies[0].wait_recv()
        far = back.at[(1 - yh) * 2 + core, :, block(j)]
        copies.append(send(far, far, to_core))

    def finish(j, copies):
        copies[1].wait_recv()
        copies[2].wait_recv()
        turned = [
            dot_nt(jnp.concatenate([back[b, k, block(j), :] for b in range(4)], axis=1), lows[k])
            for k in range(3)
        ]
        hid_part[rows(owners[j]), :] = jnp.concatenate(turned + turned[2:], axis=1).astype(bf16)

    def all_tokens(k, first=0, last=HID):
        return jnp.concatenate([back[b, k, first:last, :] for b in range(4)], axis=1)

    forward(0)
    c0 = spread(0)
    forward(1)
    c0 = cores(0, c0)
    forward(2)
    c1 = spread(1)
    c2 = spread(2)
    c0 = bend(0, c0)
    c1 = cores(1, c1)
    c2 = cores(2, c2)
    flip_back(0, 6)
    share(0, c0)
    c1 = bend(1, c1)
    c2 = bend(2, c2)
    finish(0, c0)
    for k in range(3):
        fwd_right[k].wait_recv()
        fwd_left[k].wait_recv()
    c3 = spread(3)
    share(1, c1)
    share(2, c2)
    c3 = cores(3, c3)
    finish(1, c1)
    finish(2, c2)

    def early(m, _):
        at = pl.ds(pl.multiple_of(m * SHARD, 16), SHARD)
        early_out[at, :] = dot(noisy_t[2, at, :EARLY], all_tokens(2, 0, EARLY))
        early_grad[at, :] = dot(noisy_t[0, at, :EARLY], all_tokens(0, 0, EARLY)) + dot(
            noisy_t[1, at, :EARLY], all_tokens(1, 0, EARLY)
        )
        return 0

    flip_back(6, 9)
    lax.fori_loop(0, 4, early, 0)
    c3 = bend(3, c3)
    share(3, c3)
    finish(3, c3)

    full = jnp.concatenate([dot(right_a[k], all_tokens(k)) for k in range(3)])
    ranks[...] = full.astype(bf16)
    for unit in range(NT):
        down, across = unit // 4 * 48, unit % 4 * 128
        rank_out[unit] = full[down : down + 48, across : across + 128].astype(bf16)
    r1 = [
        send(rank_out.at[peer], rank_in.at[o], {"tensor": peer})
        for o, peer in enumerate(tensor_peers)
    ]

    h1 = send(
        hid_part.at[pl.ds(pl.multiple_of((1 - core) * 576, 16), 576)], hid_core, to_core
    )

    def outputs(half, group):
        m = half * 2 + group
        at = pl.ds(pl.multiple_of(m * SHARD, 16), SHARD)
        out = early_out[at, :] + dot(noisy_t[2, at, EARLY:], all_tokens(2, EARLY))
        out = out + dot(left_c[2, at, :], ranks[128:192, :])
        grad = early_grad[at, :] + dot(noisy_t[0, at, EARLY:], all_tokens(0, EARLY))
        grad = grad + dot(noisy_t[1, at, EARLY:], all_tokens(1, EARLY))
        grad = grad + dot(left_c[0, at, :], ranks[0:64, :]) + dot(left_c[1, at, :], ranks[64:128, :])
        for i in range(4):
            cut = slice(i * OWN, (i + 1) * OWN)
            pieces[4 * m + i] = jnp.concatenate([out[cut], grad[cut]]).astype(bf16)
        return group

    def pass_on(step, half, up, copy):
        target = half * NZ + (ring(z + 4 - step, NZ) if up else ring(z - 4 + step, NZ))
        box = (up_in if up else down_in).at[step, half]
        if copy is not None:
            copy.wait_recv()
            came = (up_in if up else down_in)[step - 1, half]
            pieces[target] = (pieces[target].astype(f32) + came.astype(f32)).astype(bf16)
        return send(pieces.at[target], box, z_up if up else z_down)

    flight = {}

    def go(step, half, up):
        flight[half, up] = pass_on(step, half, up, flight.get((half, up)))

    lax.fori_loop(0, 2, outputs, 1 - z // 4)
    go(0, 0, True)
    go(0, 1, False)
    for copy in r1:
        copy.wait_recv()
    total = rank_out[tensor].astype(f32)
    for o in range(NT - 1):
        total = total + rank_in[o].astype(f32)
    rank_all[tensor] = total.astype(bf16)
    r2 = [
        send(rank_all.at[tensor], rank_all.at[tensor], {"tensor": peer}) for peer in tensor_peers
    ]
    lax.fori_loop(0, 2, outputs, z // 4)
    go(1, 1, True)
    go(1, 0, False)

    h1.wait_recv()
    own_rows = pl.ds(pl.multiple_of(core * 576 + yh * SHARD, 16), SHARD)
    far_rows = pl.ds(pl.multiple_of(core * 576 + (1 - yh) * SHARD, 16), SHARD)
    own_half = pl.ds(pl.multiple_of(yh * SHARD, 16), SHARD)
    far_half = pl.ds(pl.multiple_of((1 - yh) * SHARD, 16), SHARD)
    hid_y_out[...] = (
        hid_part[far_rows, :].astype(f32) + hid_core[far_half, :].astype(f32)
    ).astype(bf16)
    h2 = send(hid_y_out, hid_y_in, y_hi)

    go(1, 0, True)
    go(1, 1, False)

    for copy in r2:
        copy.wait_recv()
    full = jnp.concatenate(
        [jnp.concatenate([rank_all[4 * r + c] for c in range(4)], axis=1) for r in range(4)]
    )
    both = dot_nt(gathered[tensor], full)
    third = both[OWN:, 2 * RANK :]
    folded = jnp.concatenate([third[40:], jnp.zeros((8, RANK), f32)])
    folded = jnp.concatenate([third[:40], folded], axis=1)
    draw_in[x] = jnp.concatenate([both[:OWN, : 2 * RANK], folded]).astype(bf16)
    d1 = [send(draw_in.at[x], draw_in.at[x], where) for where in x_peers]

    go(2, 1, True)
    go(2, 0, False)

    h2.wait_recv()
    hid_draw[x] = (
        hid_part[own_rows, :].astype(f32)
        + hid_core[own_half, :].astype(f32)
        + hid_y_in[...].astype(f32)
    ).astype(bf16)
    h3 = [send(hid_draw.at[x], hid_draw.at[x], where) for where in x_peers]

    def over_draws(ref):
        total = (ref[0].astype(f32) + ref[1].astype(f32)) + (ref[2].astype(f32) + ref[3].astype(f32))
        return (scale_grad * total).astype(bf16)

    for copy in d1:
        copy.wait_recv()
    adapters[tensor] = over_draws(draw_in)
    mine = adapters.at[tensor]
    a1 = [
        send(mine, mine, {"tensor": yl * NZ + ring(z + o, NZ)}) for o in (1, 7, 2, 6, 3, 5, 4)
    ]
    a2 = [send(mine, mine, y_lo)]

    go(2, 0, True)
    go(2, 1, False)
    go(3, 1, True)
    go(3, 0, False)

    for copy in h3:
        copy.wait_recv()
    hid_all[own_rows, :] = over_draws(hid_draw)
    h4 = [
        send(hid_all.at[own_rows], hid_all.at[own_rows], y_hi),
        send(hid_all.at[own_rows], hid_all.at[own_rows], to_core),
    ]

    go(3, 0, True)
    go(3, 1, False)

    for o, copy in zip((1, 7, 2, 6, 3, 5, 4), a1):
        copy.wait_recv()
        at = adapters.at[yl * NZ + ring(z - o, NZ)]
        a2.append(send(at, at, y_lo))

    h4[0].wait_recv()
    h4.append(send(hid_all.at[far_rows], hid_all.at[far_rows], to_core))

    for copy in flight.values():
        copy.wait_recv()

    def over_z(half):
        return (
            pieces[half * NZ + z].astype(f32)
            + up_in[3, half].astype(f32)
            + down_in[3, half].astype(f32)
        )

    y_piece = (1 - yl) * NZ + z
    pieces[y_piece] = over_z(1 - yl).astype(bf16)
    cross = send(pieces.at[y_piece], cross_in, y_lo)
    mine = over_z(yl)
    h4[1].wait_recv()
    h4[2].wait_recv()
    turned = hid_all[...].astype(f32).T
    right_ref[0] = turned[:RANK].astype(bf16)
    right_ref[1] = turned[RANK : 2 * RANK].astype(bf16)
    down_left_ref[...] = turned[2 * RANK : 3 * RANK].astype(bf16)
    cross.wait_recv()
    mine = mine + cross_in[...].astype(f32)
    out_ref[...] = mine[:OWN].astype(bf16)
    grad_ref[...] = mine[OWN:].astype(bf16)
    for copy in a2:
        copy.wait_recv()
    for t in range(NT):
        both = adapters[t].astype(f32)
        tall[0, t * OWN : (t + 1) * OWN, :] = both[:OWN]
        tall[1, t * OWN : t * OWN + 40, :RANK] = both[OWN:, :RANK]
        tall[1, t * OWN + 40 : (t + 1) * OWN, :RANK] = both[OWN : OWN + 32, RANK:]
    turned = tall[0].T.astype(bf16)
    left_ref[0] = turned[:RANK]
    left_ref[1] = turned[RANK:]
    down_right_ref[...] = tall[1].T[:RANK].astype(bf16)
    for copy in started:
        copy.wait_send()


def hand_over(*refs):
    for source, target in zip(refs[:6], refs[6:]):
        target[...] = source[...]


def on_device(
    tokens,
    cotangent,
    gate_up_weight,
    down_weight,
    gate_up_noise,
    down_noise,
    gate_up_left,
    gate_up_right,
    down_left,
    down_right,
):
    scale_grad = (NX * TOK) ** (-0.5)
    vmem, anywhere = pl.BlockSpec(memory_space=pltpu.VMEM), pl.BlockSpec(memory_space=pl.ANY)
    scratch = [
        pltpu.VMEM((3, HID, FEAT), bf16),
        pltpu.VMEM((3, HID, FEAT), bf16),
        pltpu.VMEM((3, FEAT, HID), bf16),
        pltpu.VMEM((NT, 2 * OWN, TOK), bf16),
        pltpu.VMEM((2, FEAT, TOK), bf16),
        pltpu.VMEM((3, FEAT, RANK), bf16),
        pltpu.VMEM((3, HID, RANK), bf16),
        pltpu.VMEM((3, RANK, HID), bf16),
        pltpu.VMEM((3, RANK, TOK), bf16),
        pltpu.VMEM((3 * RANK, TOK), bf16),
        pltpu.VMEM((NX, 2, 2, 3, SHARD, LANES), bf16),
        pltpu.VMEM((NX, 2, 3, SHARD, LANES), bf16),
        pltpu.VMEM((NX, 3, SHARD, LANES), bf16),
        pltpu.VMEM((NX, 3, SHARD, LANES), bf16),
        pltpu.VMEM((4, 3, HID, LANES), bf16),
        pltpu.VMEM((FEAT, TOK), f32),
        pltpu.VMEM((FEAT, TOK), f32),
        pltpu.VMEM((NT, 2 * OWN, TOK), bf16),
        pltpu.VMEM((4, 2, 2 * OWN, TOK), bf16),
        pltpu.VMEM((4, 2, 2 * OWN, TOK), bf16),
        pltpu.VMEM((2 * OWN, TOK), bf16),
        pltpu.VMEM((NT, 48, 128), bf16),
        pltpu.VMEM((NT, 48, 128), bf16),
        pltpu.VMEM((NT, 48, 128), bf16),
        pltpu.VMEM((NX, PACK, 2 * RANK), bf16),
        pltpu.VMEM((NT, PACK, 2 * RANK), bf16),
        pltpu.VMEM((2, FEAT, 2 * RANK), f32),
        pltpu.VMEM((HID, 4 * RANK), bf16),
        pltpu.VMEM((HID // 2, 4 * RANK), bf16),
        pltpu.VMEM((SHARD, 4 * RANK), bf16),
        pltpu.VMEM((SHARD, 4 * RANK), bf16),
        pltpu.VMEM((NX, SHARD, 4 * RANK), bf16),
        pltpu.VMEM((HID, 4 * RANK), bf16),
        pltpu.SemaphoreType.DMA((MESSAGES,)),
        pltpu.SemaphoreType.DMA((MESSAGES,)),
        pltpu.SemaphoreType.DMA((10,)),
    ]
    shapes = [
        (OWN, TOK),
        (OWN, TOK),
        (2, RANK, FEAT),
        (2, RANK, HID),
        (RANK, HID),
        (RANK, FEAT),
    ]
    shapes = tuple(jax.ShapeDtypeStruct(shape, bf16) for shape in shapes)
    results = pl.pallas_call(
        functools.partial(kernel, scale_grad),
        out_shape=shapes,
        in_specs=[vmem] * 2 + [anywhere] * 4 + [vmem] * 4,
        out_specs=(vmem,) * 6,
        scratch_shapes=scratch,
        compiler_params=pltpu.CompilerParams(
            collective_id=0, has_side_effects=True, vmem_limit_bytes=62 * 2**20
        ),
    )(
        tokens[0].T,
        cotangent[0].T,
        jnp.swapaxes(gate_up_weight, 1, 2),
        down_weight,
        gate_up_noise[0],
        down_noise[0],
        jnp.swapaxes(gate_up_left, 1, 2),
        gate_up_right,
        down_left.T,
        down_right,
    )
    out, grad, left, right, down_left_grad, down_right_grad = pl.pallas_call(
        hand_over, out_shape=shapes, in_specs=[vmem] * 6, out_specs=(vmem,) * 6
    )(*results)
    return (
        out.T[None],
        grad.T[None],
        jnp.swapaxes(left, 1, 2),
        right,
        down_left_grad.T,
        down_right_grad,
    )


def solution(mesh):
    in_specs = (
        P("draw", None, ("batch", "tensor")),
        P("draw", None, ("batch", "tensor")),
        P(None, "batch", ("tensor", "draw")),
        P(("tensor", "draw"), "batch"),
        P("draw", None, "batch", "tensor"),
        P("draw", "tensor", "batch"),
        P(None, "batch", None),
        P(None, None, "tensor"),
        P("tensor", None),
        P(None, "batch"),
    )
    out_specs = (
        P("draw", None, ("batch", "tensor")),
        P("draw", None, ("batch", "tensor")),
        P(None, "batch", None),
        P(None, None, "tensor"),
        P("tensor", None),
        P(None, "batch"),
    )
    return jax.shard_map(
        on_device, mesh=mesh, in_specs=in_specs, out_specs=out_specs, check_vma=False
    )
```

```python
import functools

import jax
import jax.numpy as jnp
from jax import lax
from jax.experimental import pallas as pl
from jax.experimental.pallas import tpu as pltpu
from jax.sharding import PartitionSpec as P

MESH = pl.DeviceIdType.MESH
f32, bf16 = jnp.float32, jnp.bfloat16

noise_sigma = 0.5
root_coeff = 0.7978845608028654
cubic_coeff = 0.044715

FEAT, HID, TOK, RANK = 1152, 1152, 512, 64
NX, NZ, NT = 4, 8, 16
SHARD = HID // NX
HALF = SHARD // 2
OWN = FEAT // NT
PACK = OWN + 40
LANES = TOK // 4
PARTS = ((0, 80), (80, 64), (144, 80), (224, 64))
PLACES = ((0, 80, 144, 224), (720, 800, 432, 512), (864, 1024, 944, 1088), (288, 368, 576, 656))
BLOCKS = (
    (0, 288, ((0, 0, 288),)),
    (288, 288, ((3, 0, 144), (1, 144, 144))),
    (576, 288, ((3, 144, 144), (1, 0, 144))),
    (864, 160, ((2, 0, 80), (2, 144, 80))),
    (1024, 128, ((2, 80, 64), (2, 224, 64))),
)
HALFT = TOK // 2
EARLY = 768
MESSAGES = 180


def gelu_pair(value):
    inner = root_coeff * (value + cubic_coeff * value * value * value)
    bend = jnp.tanh(inner)
    result = 0.5 * value * (1.0 + bend)
    slope = 0.5 * (1.0 + bend) + 0.5 * value * (1.0 - bend * bend) * root_coeff * (
        1.0 + 3.0 * cubic_coeff * value * value
    )
    return (result, slope)


def dot(left, right):
    return jnp.dot(left, right, preferred_element_type=f32)


def dot_nt(left, right):
    return lax.dot_general(left, right, (((1,), (1,)), ((), ())), preferred_element_type=f32)


def kernel(
    scale_grad,
    tokens_in,
    cotangent_in,
    wgu_in,
    wdn_in,
    ngu_in,
    ndn_in,
    left_t,
    right_n,
    down_left_t,
    down_right_n,
    out_ref,
    grad_ref,
    left_ref,
    right_ref,
    down_left_ref,
    down_right_ref,
    weights,
    noisy,
    noisy_t,
    own_acts,
    gathered,
    gathered_c,
    acts,
    left_c,
    right_c,
    right_a,
    lows,
    ranks,
    part,
    core_in,
    y_out,
    y_in,
    back,
    early_out,
    early_grad,
    pieces,
    up_in,
    down_in,
    cross_in,
    y_pieces,
    y_pieces_in,
    y_up_in,
    y_down_in,
    rank_out,
    rank_in,
    rank_all,
    draw_in,
    adapters,
    tall,
    hid_part,
    hid_core,
    hid_y_out,
    hid_y_in,
    hid_draw,
    hid_all,
    send_sem,
    recv_sem,
    local_sem,
):
    tensor = lax.axis_index("tensor")
    x = lax.axis_index("draw")
    batch = lax.axis_index("batch")
    yl, z = tensor // NZ, tensor % NZ
    yh, core = batch // 2, batch % 2

    def ring(value, count):
        return (value + count) % count

    x_peers = [{"draw": ring(x + o, NX)} for o in (1, 2, 3)]
    x_right, x_left = x_peers[0], x_peers[2]
    z_up = {"tensor": yl * NZ + ring(z + 1, NZ)}
    z_down = {"tensor": yl * NZ + ring(z - 1, NZ)}
    y_lo = {"tensor": (1 - yl) * NZ + z}
    to_core = {"batch": yh * 2 + 1 - core}
    y_hi = {"batch": (1 - yh) * 2 + core}

    count = [0]
    started = []

    def send(src, dst, where):
        at = count[0]
        count[0] += 1
        assert at < MESSAGES
        copy = pltpu.make_async_remote_copy(
            src_ref=src,
            dst_ref=dst,
            send_sem=send_sem.at[at],
            recv_sem=recv_sem.at[at],
            device_id=where,
            device_id_type=MESH,
        )
        copy.start()
        started.append(copy)
        return copy

    def side_by_side(value):
        return jnp.concatenate([value[:, :HALFT], value[:, HALFT:]])

    own_tokens, own_cotangent = tokens_in[...].astype(f32), cotangent_in[...].astype(f32)
    own_acts[...] = jnp.concatenate([own_tokens, own_cotangent]).astype(bf16)
    gathered[tensor] = side_by_side(own_tokens).astype(bf16)
    gathered_c[tensor] = side_by_side(own_cotangent).astype(bf16)

    barrier = pltpu.get_barrier_semaphore()
    tensor_peers = [(tensor + o) % NT for o in range(1, NT)]
    partners = [*x_peers, to_core, y_hi, *({"tensor": peer} for peer in tensor_peers)]
    for where in partners:
        pl.semaphore_signal(barrier, inc=1, device_id=where, device_id_type=MESH)
    pl.semaphore_wait(barrier, len(partners))

    def rows(owner, first=0, size=SHARD):
        return pl.ds(pl.multiple_of(owner * SHARD + first, 16), size)

    owners = [x, ring(x + 1, NX), ring(x + 2, NX), ring(x - 1, NX)]

    def place(owner, piece):
        away = ring(owner - x, NX)
        odd, high = away % 2, away // 2
        right, opposite, left = odd * (1 - high), (1 - odd) * high, odd * high
        first = PLACES[0][piece] * (1 - right - opposite - left) + PLACES[1][piece] * right
        first = first + PLACES[2][piece] * opposite + PLACES[3][piece] * left
        return pl.ds(pl.multiple_of(first, 16), PARTS[piece][1])

    def block(j):
        return pl.ds(BLOCKS[j][0], BLOCKS[j][1])

    y_copy = send(gathered.at[tensor], gathered.at[tensor], y_lo)
    y_copy_c = send(gathered_c.at[tensor], gathered_c.at[tensor], y_lo)
    to_right, to_left = [], []

    def own_shard(half, k):
        source = wgu_in.at[k] if k < 2 else wdn_in
        for flight, turn, where in ((to_right, half, x_right), (to_left, 1 - half, x_left)):
            first = turn * HALF
            flight.append(
                send(source.at[pl.ds(first, HALF)], weights.at[k, rows(x, first, HALF)], where)
            )

    for half in (0, 1):
        for k in (0, 1):
            own_shard(half, k)
    locals_ = [
        pltpu.make_async_copy(ngu_in.at[0], noisy_t.at[0], local_sem.at[1]),
        pltpu.make_async_copy(ngu_in.at[1], noisy_t.at[1], local_sem.at[2]),
        pltpu.make_async_copy(wgu_in.at[0], weights.at[0, rows(x)], local_sem.at[3]),
        pltpu.make_async_copy(wgu_in.at[1], weights.at[1, rows(x)], local_sem.at[4]),
        pltpu.make_async_copy(wdn_in, weights.at[2, rows(x)], local_sem.at[5]),
    ]
    spans = []
    for start, _, parts in BLOCKS:
        for shard, first, size in parts:
            spans.append((start, shard, first, size))
            start += size
    locals_ += [
        pltpu.make_async_copy(
            ndn_in.at[rows(owners[shard], first, size)],
            noisy.at[2, pl.ds(start, size)],
            local_sem.at[6 + at],
        )
        for at, (start, shard, first, size) in enumerate(spans)
    ]
    for copy in locals_:
        copy.start()

    def gather_rings(ref):
        def hop(step, half, up):
            at = half * NZ + (ring(z - step, NZ) if up else ring(z + step, NZ))
            return send(ref.at[at], ref.at[at], z_up if up else z_down)

        flight = {}
        for half in (0, 1):
            for up in (True, False):
                flight[half, up] = hop(0, half, up)
        yield 0
        for step in (1, 2, 3, 4):
            for half in (0, 1):
                for up in (True, False):
                    last = 4 if (half == 0) == up else 3
                    if step > last:
                        continue
                    flight[half, up].wait_recv()
                    if step < last:
                        flight[half, up] = hop(step, half, up)
            yield step

    def flip_noise(first, last):
        def body(strip, _):
            k, at = strip // 9, pl.ds(pl.multiple_of((strip % 9) * 128, 128), 128)
            turned = noisy_t[k, at, :].T
            for i in range(NX):
                for piece, (first, size) in enumerate(PARTS):
                    first += i * SHARD
                    noisy[k, place(i, piece), at] = turned[first : first + size]
            return 0

        lax.fori_loop(first, last, body, 0)

    def flip_back(k_first, k_last, first, last):
        many = last - first

        def body(strip, _):
            k = k_first + strip // many
            at = pl.ds(pl.multiple_of((first + strip % many) * 128, 128), 128)
            noisy_t[k, :, at] = noisy[k, at, :].T
            return 0

        lax.fori_loop(0, (k_last - k_first) * many, body, 0)

    for k in range(3):
        left_c[k] = (left_t[k] if k < 2 else down_right_n[...]).T
        turned = (right_n[k] if k < 2 else down_left_t[...]).T
        for i in range(NX):
            for piece, (first, size) in enumerate(PARTS):
                first += i * SHARD
                right_c[k, place(i, piece), :] = turned[first : first + size]
        right_a[k] = right_c[k].T
    y_copy.wait_recv()
    rings = gather_rings(gathered)
    next(rings)
    locals_[0].wait()
    locals_[1].wait()
    flip_noise(0, 9)
    next(rings)
    flip_noise(9, 18)
    next(rings)
    next(rings)
    next(rings)
    y_copy_c.wait_recv()
    rings = gather_rings(gathered_c)
    next(rings)

    def unpack(source, target):
        def body(m, _):
            one, two = source[2 * m].astype(f32), source[2 * m + 1].astype(f32)
            at = pl.ds(pl.multiple_of(m * 2 * OWN, 16), 2 * OWN)
            acts[target, at, :HALFT] = jnp.concatenate([one[:OWN], two[:OWN]]).astype(bf16)
            acts[target, at, HALFT:] = jnp.concatenate([one[OWN:], two[OWN:]]).astype(bf16)
            return 0

        lax.fori_loop(0, NZ, body, 0)

    x_l, x_r = owners[3], owners[1]
    last = []

    def forward(k, first, size):
        at = weights.at[k, rows(x_l, first, size)]
        last.append(send(at, at, x_right))
        at = weights.at[k, rows(x_r, first + HALF, size)]
        last.append(send(at, at, x_left))

    def spread(j, k_first, k_last):
        start, size, parts = BLOCKS[j]

        def body(k, _):
            at = start
            for shard, first, count in parts:
                here = pl.ds(at, count)
                noisy[k, here, :] = (
                    weights[k, rows(owners[shard], first, count), :].astype(f32)
                    * (1.0 + noise_sigma * noisy[k, here, :].astype(f32))
                ).astype(bf16)
                at += count
            total = dot(noisy[k, block(j), :], acts[k // 2])
            total = total + dot(right_c[k, block(j), :], lows[k])
            for b in range(4):
                part[b % 2, b // 2, k, block(j), :] = total[:, b * LANES : (b + 1) * LANES].astype(
                    bf16
                )
            return 0

        lax.fori_loop(k_first, k_last, body, 0)
        ks = pl.ds(k_first, k_last - k_first)
        return send(part.at[1 - core, :, ks, block(j)], core_in.at[:, ks, block(j)], to_core)

    def cores(j, k_first, k_last, copy):
        copy.wait_recv()
        at, ks = block(j), pl.ds(k_first, k_last - k_first)
        for half in (0, 1):
            for k in range(k_first, k_last):
                y_out[half, k, at, :] = (
                    part[core, half, k, at, :].astype(f32) + core_in[half, k, at, :].astype(f32)
                ).astype(bf16)
        return send(y_out.at[:, ks, at], y_in.at[:, ks, at], y_hi)

    def whole(half, k, at):
        return y_out[half, k, at, :].astype(f32) + y_in[half, k, at, :].astype(f32)

    def bend(j, copy):
        copy.wait_recv()
        at = block(j)
        for half in (0, 1):
            active, _ = gelu_pair(whole(half, 0, at))
            back[core, half, 2, at, :] = (active * whole(half, 1, at)).astype(bf16)
        mine = back.at[core, :, 2, at]
        return send(mine, mine, to_core)

    def bend_grad(j, copy):
        copy.wait_recv()
        at = block(j)
        for half in (0, 1):
            active, slope = gelu_pair(whole(half, 0, at))
            grad = whole(half, 2, at)
            back[core, half, 0, at, :] = (grad * whole(half, 1, at) * slope).astype(bf16)
            back[core, half, 1, at, :] = (grad * active).astype(bf16)
        mine = back.at[core, :, pl.ds(0, 2), at]
        return send(mine, mine, to_core)

    def all_tokens(k, first=0, last=HID):
        return jnp.concatenate([back[b % 2, b // 2, k, first:last, :] for b in range(4)], axis=1)

    def hid_rows(j, ks, lanes):
        start, size, parts = BLOCKS[j]
        turned = [dot_nt(all_tokens(k, start, start + size), lows[k]) for k in ks]
        turned = jnp.concatenate(turned, axis=1).astype(bf16)
        at = 0
        for shard, first, count in parts:
            hid_part[rows(owners[shard], first, count), lanes] = turned[at : at + count]
            at += count

    def finish(j, copy):
        copy.wait_recv()
        hid_rows(j, (2, 2), slice(2 * RANK, 4 * RANK))

    def finish_grad(j, copy):
        copy.wait_recv()
        hid_rows(j, (0, 1), slice(0, 2 * RANK))

    def early_outputs(m, _):
        at = pl.ds(pl.multiple_of(m * SHARD, 16), SHARD)
        early_out[at, :] = dot(noisy_t[2, at, :EARLY], all_tokens(2, 0, EARLY))
        return 0

    def early_grads(m, _):
        at = pl.ds(pl.multiple_of(m * SHARD, 16), SHARD)
        early_grad[at, :] = dot(noisy_t[0, at, :EARLY], all_tokens(0, 0, EARLY)) + dot(
            noisy_t[1, at, :EARLY], all_tokens(1, 0, EARLY)
        )
        return 0

    for k in (0, 1):
        to_right[k].wait_recv()
        to_left[k].wait_recv()
    for k in (0, 1):
        forward(k, 0, 80)
    for k in (0, 1):
        forward(k, 80, 64)
    own_shard(0, 2)
    own_shard(1, 2)
    unpack(gathered, 0)
    lows[0] = dot(left_t[0], acts[0]).astype(bf16)
    lows[1] = dot(left_t[1], acts[0]).astype(bf16)
    for copy in locals_[2:]:
        copy.wait()
    g0 = spread(0, 0, 2)
    g1 = spread(1, 0, 2)
    next(rings)
    g0 = cores(0, 0, 2, g0)
    g1 = cores(1, 0, 2, g1)
    next(rings)
    for k in (2, 3):
        to_right[k].wait_recv()
        to_left[k].wait_recv()
    g2 = spread(2, 0, 2)
    next(rings)
    g2 = cores(2, 0, 2, g2)
    next(rings)
    unpack(gathered_c, 1)
    lows[2] = dot(down_right_n[...], acts[1]).astype(bf16)
    d0 = spread(0, 2, 3)
    g0 = bend(0, g0)
    d0 = cores(0, 2, 3, d0)
    for copy in last[:4]:
        copy.wait_recv()
    g3 = spread(3, 0, 2)
    flip_back(0, 2, 0, 6)
    g3 = cores(3, 0, 2, g3)
    g1 = bend(1, g1)
    finish(0, g0)
    for copy in last[4:8]:
        copy.wait_recv()
    g4 = spread(4, 0, 2)
    finish(1, g1)
    g4 = cores(4, 0, 2, g4)
    flip_back(0, 2, 6, 9)
    g2 = bend(2, g2)
    to_right[4].wait_recv()
    to_left[4].wait_recv()
    forward(2, 0, 80)
    forward(2, 80, 64)
    d1 = spread(1, 2, 3)
    d0 = bend_grad(0, d0)
    finish(2, g2)
    d1 = cores(1, 2, 3, d1)
    g3 = bend(3, g3)
    finish_grad(0, d0)
    finish(3, g3)
    to_right[5].wait_recv()
    to_left[5].wait_recv()
    d2 = spread(2, 2, 3)
    g4 = bend(4, g4)
    d2 = cores(2, 2, 3, d2)
    flip_back(2, 3, 0, 6)
    lax.fori_loop(0, 4, early_outputs, 0)
    finish(4, g4)
    for copy in last[8:10]:
        copy.wait_recv()
    d3 = spread(3, 2, 3)
    d1 = bend_grad(1, d1)
    ranks[pl.ds(2 * RANK, RANK), :] = dot(right_a[2], all_tokens(2)).astype(bf16)
    d3 = cores(3, 2, 3, d3)
    for copy in last[10:]:
        copy.wait_recv()
    d4 = spread(4, 2, 3)
    flip_back(2, 3, 6, 9)
    d4 = cores(4, 2, 3, d4)

    def outputs(half, group):
        m = half * 2 + group
        at = pl.ds(pl.multiple_of(m * SHARD, 16), SHARD)
        out = early_out[at, :] + dot(noisy_t[2, at, EARLY:], all_tokens(2, EARLY))
        out = out + dot(left_c[2, at, :], ranks[128:192, :])
        for i in range(4):
            pieces[4 * m + i] = side_by_side(out[i * OWN : (i + 1) * OWN]).astype(bf16)
        return group

    def pass_on(step, half, up, copy):
        target = half * NZ + (ring(z + 4 - step, NZ) if up else ring(z - 4 + step, NZ))
        box = (up_in if up else down_in).at[step, half]
        if copy is not None:
            copy.wait_recv()
            came = (up_in if up else down_in)[step - 1, half]
            pieces[target] = (pieces[target].astype(f32) + came.astype(f32)).astype(bf16)
        return send(pieces.at[target], box, z_up if up else z_down)

    flight = {}

    def go(step, half, up):
        flight[half, up] = pass_on(step, half, up, flight.get((half, up)))

    lax.fori_loop(0, 2, outputs, 1 - z // 4)
    go(0, 0, True)
    go(0, 1, False)
    lax.fori_loop(0, 2, outputs, z // 4)
    go(1, 1, True)
    go(1, 0, False)
    d2 = bend_grad(2, d2)
    finish_grad(1, d1)
    finish_grad(2, d2)
    d3 = bend_grad(3, d3)
    go(1, 0, True)
    go(1, 1, False)
    lax.fori_loop(0, 4, early_grads, 0)
    d4 = bend_grad(4, d4)
    finish_grad(3, d3)
    finish_grad(4, d4)

    full = jnp.concatenate([dot(right_a[k], all_tokens(k)) for k in (0, 1)]).astype(bf16)
    ranks[: 2 * RANK, :] = full
    full = jnp.concatenate([full, ranks[2 * RANK :, :]])
    for unit in range(NT):
        down, across = unit // 4 * 48, unit % 4 * 128
        rank_out[unit] = full[down : down + 48, across : across + 128]
    r1 = [
        send(rank_out.at[peer], rank_in.at[o], {"tensor": peer})
        for o, peer in enumerate(tensor_peers)
    ]

    h1 = send(
        hid_part.at[pl.ds(pl.multiple_of((1 - core) * 576, 16), 576)], hid_core, to_core
    )

    def grads(half, group):
        m = half * 2 + group
        at = pl.ds(pl.multiple_of(m * SHARD, 16), SHARD)
        grad = early_grad[at, :] + dot(noisy_t[0, at, EARLY:], all_tokens(0, EARLY))
        grad = grad + dot(noisy_t[1, at, EARLY:], all_tokens(1, EARLY))
        grad = grad + dot(left_c[0, at, :], ranks[0:64, :]) + dot(left_c[1, at, :], ranks[64:128, :])
        for i in range(4):
            y_pieces[4 * m + i] = side_by_side(grad[i * OWN : (i + 1) * OWN]).astype(bf16)
        return group

    def cross_y(target):
        at = (1 - yl) * NZ + ring(target, NZ)
        return send(y_pieces.at[at], y_pieces_in.at[ring(target, NZ)], y_lo)

    def y_pass(step, up, copy, arrived):
        target = ring(z + 4 - step, NZ) if up else ring(z - 3 + step, NZ)
        box = y_up_in if up else y_down_in
        arrived.wait_recv()
        total = y_pieces[yl * NZ + target].astype(f32) + y_pieces_in[target].astype(f32)
        if copy is not None:
            copy.wait_recv()
            total = total + box[step - 1].astype(f32)
        y_pieces[yl * NZ + target] = total.astype(bf16)
        return send(y_pieces.at[yl * NZ + target], box.at[step], z_up if up else z_down)

    lax.fori_loop(0, 2, grads, 1 - z // 4)
    crossed = {4: cross_y(z + 4)}
    go(2, 1, True)
    go(2, 0, False)
    lax.fori_loop(0, 2, grads, z // 4)
    for away in (3, -3, 2, -2, 1, -1, 0):
        crossed[away] = cross_y(z + away)
    go(2, 0, True)
    go(2, 1, False)
    for copy in r1:
        copy.wait_recv()
    total = rank_out[tensor].astype(f32)
    for o in range(NT - 1):
        total = total + rank_in[o].astype(f32)
    rank_all[tensor] = total.astype(bf16)
    r2 = [
        send(rank_all.at[tensor], rank_all.at[tensor], {"tensor": peer}) for peer in tensor_peers
    ]
    y_up = y_pass(0, True, None, crossed[4])
    go(3, 1, True)
    go(3, 0, False)

    h1.wait_recv()
    own_rows = pl.ds(pl.multiple_of(core * 576 + yh * SHARD, 16), SHARD)
    far_rows = pl.ds(pl.multiple_of(core * 576 + (1 - yh) * SHARD, 16), SHARD)
    own_half = pl.ds(pl.multiple_of(yh * SHARD, 16), SHARD)
    far_half = pl.ds(pl.multiple_of((1 - yh) * SHARD, 16), SHARD)
    hid_y_out[...] = (
        hid_part[far_rows, :].astype(f32) + hid_core[far_half, :].astype(f32)
    ).astype(bf16)
    h2 = send(hid_y_out, hid_y_in, y_hi)

    y_down = y_pass(0, False, None, crossed[-3])
    go(3, 0, True)
    go(3, 1, False)
    y_up = y_pass(1, True, y_up, crossed[3])

    for copy in r2:
        copy.wait_recv()
    full = jnp.concatenate(
        [jnp.concatenate([rank_all[4 * r + c] for c in range(4)], axis=1) for r in range(4)]
    )
    both = dot_nt(own_acts[...], full)
    third = both[OWN:, 2 * RANK :]
    folded = jnp.concatenate([third[40:], jnp.zeros((8, RANK), f32)])
    folded = jnp.concatenate([third[:40], folded], axis=1)
    draw_in[x] = jnp.concatenate([both[:OWN, : 2 * RANK], folded]).astype(bf16)
    d1 = [send(draw_in.at[x], draw_in.at[x], where) for where in x_peers]

    for copy in flight.values():
        copy.wait_recv()

    def over_z(half):
        return (
            pieces[half * NZ + z].astype(f32)
            + up_in[3, half].astype(f32)
            + down_in[3, half].astype(f32)
        )

    y_piece = (1 - yl) * NZ + z
    pieces[y_piece] = over_z(1 - yl).astype(bf16)
    cross = send(pieces.at[y_piece], cross_in, y_lo)
    y_down = y_pass(1, False, y_down, crossed[-2])
    y_up = y_pass(2, True, y_up, crossed[2])

    def over_draws(ref):
        total = (ref[0].astype(f32) + ref[1].astype(f32)) + (ref[2].astype(f32) + ref[3].astype(f32))
        return (scale_grad * total).astype(bf16)

    for copy in d1:
        copy.wait_recv()
    adapters[tensor] = over_draws(draw_in)
    mine = adapters.at[tensor]
    a1 = [
        send(mine, mine, {"tensor": yl * NZ + ring(z + o, NZ)}) for o in (1, 7, 2, 6, 3, 5, 4)
    ]
    a2 = [send(mine, mine, y_lo)]

    y_down = y_pass(2, False, y_down, crossed[-1])
    y_up = y_pass(3, True, y_up, crossed[1])

    h2.wait_recv()
    hid_draw[x] = (
        hid_part[own_rows, :].astype(f32)
        + hid_core[own_half, :].astype(f32)
        + hid_y_in[...].astype(f32)
    ).astype(bf16)
    h3 = [send(hid_draw.at[x], hid_draw.at[x], where) for where in x_peers]

    cross.wait_recv()
    first = over_z(yl) + cross_in[...].astype(f32)
    out_ref[:, :HALFT] = first[:OWN].astype(bf16)
    out_ref[:, HALFT:] = first[OWN:].astype(bf16)
    for o, copy in zip((1, 7, 2, 6, 3, 5, 4), a1):
        copy.wait_recv()
        at = adapters.at[yl * NZ + ring(z - o, NZ)]
        a2.append(send(at, at, y_lo))

    for copy in h3:
        copy.wait_recv()
    hid_all[own_rows, :] = over_draws(hid_draw)
    h4 = [
        send(hid_all.at[own_rows], hid_all.at[own_rows], y_hi),
        send(hid_all.at[own_rows], hid_all.at[own_rows], to_core),
    ]
    y_up.wait_recv()
    y_down.wait_recv()
    crossed[0].wait_recv()
    second = (
        (y_pieces[yl * NZ + z].astype(f32) + y_pieces_in[z].astype(f32))
        + y_up_in[3].astype(f32)
        + y_down_in[2].astype(f32)
    )
    grad_ref[:, :HALFT] = second[:OWN].astype(bf16)
    grad_ref[:, HALFT:] = second[OWN:].astype(bf16)
    h4[0].wait_recv()
    h4.append(send(hid_all.at[far_rows], hid_all.at[far_rows], to_core))
    for copy in a2:
        copy.wait_recv()
    for t in range(NT):
        both = adapters[t].astype(f32)
        tall[0, t * OWN : (t + 1) * OWN, :] = both[:OWN]
        tall[1, t * OWN : t * OWN + 40, :RANK] = both[OWN:, :RANK]
        tall[1, t * OWN + 40 : (t + 1) * OWN, :RANK] = both[OWN : OWN + 32, RANK:]
    turned = tall[0].T.astype(bf16)
    left_ref[0] = turned[:RANK]
    left_ref[1] = turned[RANK:]
    down_right_ref[...] = tall[1].T[:RANK].astype(bf16)
    h4[1].wait_recv()
    h4[2].wait_recv()
    turned = hid_all[...].astype(f32).T
    right_ref[0] = turned[:RANK].astype(bf16)
    right_ref[1] = turned[RANK : 2 * RANK].astype(bf16)
    down_left_ref[...] = turned[2 * RANK : 3 * RANK].astype(bf16)
    for copy in started:
        copy.wait_send()


def hand_over(*refs):
    for source, target in zip(refs[:6], refs[6:]):
        target[...] = source[...]


def on_device(
    tokens,
    cotangent,
    gate_up_weight,
    down_weight,
    gate_up_noise,
    down_noise,
    gate_up_left,
    gate_up_right,
    down_left,
    down_right,
):
    scale_grad = (NX * TOK) ** (-0.5)
    vmem, anywhere = pl.BlockSpec(memory_space=pltpu.VMEM), pl.BlockSpec(memory_space=pl.ANY)
    scratch = [
        pltpu.VMEM((3, HID, FEAT), bf16),
        pltpu.VMEM((3, HID, FEAT), bf16),
        pltpu.VMEM((3, FEAT, HID), bf16),
        pltpu.VMEM((2 * OWN, TOK), bf16),
        pltpu.VMEM((NT, 2 * OWN, HALFT), bf16),
        pltpu.VMEM((NT, 2 * OWN, HALFT), bf16),
        pltpu.VMEM((2, FEAT, TOK), bf16),
        pltpu.VMEM((3, FEAT, RANK), bf16),
        pltpu.VMEM((3, HID, RANK), bf16),
        pltpu.VMEM((3, RANK, HID), bf16),
        pltpu.VMEM((3, RANK, TOK), bf16),
        pltpu.VMEM((3 * RANK, TOK), bf16),
        pltpu.VMEM((2, 2, 3, HID, LANES), bf16),
        pltpu.VMEM((2, 3, HID, LANES), bf16),
        pltpu.VMEM((2, 3, HID, LANES), bf16),
        pltpu.VMEM((2, 3, HID, LANES), bf16),
        pltpu.VMEM((2, 2, 3, HID, LANES), bf16),
        pltpu.VMEM((FEAT, TOK), f32),
        pltpu.VMEM((FEAT, TOK), f32),
        pltpu.VMEM((NT, 2 * OWN, HALFT), bf16),
        pltpu.VMEM((4, 2, 2 * OWN, HALFT), bf16),
        pltpu.VMEM((4, 2, 2 * OWN, HALFT), bf16),
        pltpu.VMEM((2 * OWN, HALFT), bf16),
        pltpu.VMEM((NT, 2 * OWN, HALFT), bf16),
        pltpu.VMEM((NZ, 2 * OWN, HALFT), bf16),
        pltpu.VMEM((4, 2 * OWN, HALFT), bf16),
        pltpu.VMEM((3, 2 * OWN, HALFT), bf16),
        pltpu.VMEM((NT, 48, 128), bf16),
        pltpu.VMEM((NT, 48, 128), bf16),
        pltpu.VMEM((NT, 48, 128), bf16),
        pltpu.VMEM((NX, PACK, 2 * RANK), bf16),
        pltpu.VMEM((NT, PACK, 2 * RANK), bf16),
        pltpu.VMEM((2, FEAT, 2 * RANK), f32),
        pltpu.VMEM((HID, 4 * RANK), bf16),
        pltpu.VMEM((HID // 2, 4 * RANK), bf16),
        pltpu.VMEM((SHARD, 4 * RANK), bf16),
        pltpu.VMEM((SHARD, 4 * RANK), bf16),
        pltpu.VMEM((NX, SHARD, 4 * RANK), bf16),
        pltpu.VMEM((HID, 4 * RANK), bf16),
        pltpu.SemaphoreType.DMA((MESSAGES,)),
        pltpu.SemaphoreType.DMA((MESSAGES,)),
        pltpu.SemaphoreType.DMA((16,)),
    ]
    shapes = [
        (OWN, TOK),
        (OWN, TOK),
        (2, RANK, FEAT),
        (2, RANK, HID),
        (RANK, HID),
        (RANK, FEAT),
    ]
    shapes = tuple(jax.ShapeDtypeStruct(shape, bf16) for shape in shapes)
    results = pl.pallas_call(
        functools.partial(kernel, scale_grad),
        out_shape=shapes,
        in_specs=[vmem] * 2 + [anywhere] * 4 + [vmem] * 4,
        out_specs=(vmem,) * 6,
        scratch_shapes=scratch,
        compiler_params=pltpu.CompilerParams(
            collective_id=0, has_side_effects=True, vmem_limit_bytes=62 * 2**20
        ),
    )(
        tokens[0].T,
        cotangent[0].T,
        jnp.swapaxes(gate_up_weight, 1, 2),
        down_weight,
        gate_up_noise[0],
        down_noise[0],
        jnp.swapaxes(gate_up_left, 1, 2),
        gate_up_right,
        down_left.T,
        down_right,
    )
    out, grad, left, right, down_left_grad, down_right_grad = pl.pallas_call(
        hand_over, out_shape=shapes, in_specs=[vmem] * 6, out_specs=(vmem,) * 6
    )(*results)
    return (
        out.T[None],
        grad.T[None],
        jnp.swapaxes(left, 1, 2),
        right,
        down_left_grad.T,
        down_right_grad,
    )


def solution(mesh):
    in_specs = (
        P("draw", None, ("batch", "tensor")),
        P("draw", None, ("batch", "tensor")),
        P(None, "batch", ("tensor", "draw")),
        P(("tensor", "draw"), "batch"),
        P("draw", None, "batch", "tensor"),
        P("draw", "tensor", "batch"),
        P(None, "batch", None),
        P(None, None, "tensor"),
        P("tensor", None),
        P(None, "batch"),
    )
    out_specs = (
        P("draw", None, ("batch", "tensor")),
        P("draw", None, ("batch", "tensor")),
        P(None, "batch", None),
        P(None, None, "tensor"),
        P("tensor", None),
        P(None, "batch"),
    )
    return jax.shard_map(
        on_device, mesh=mesh, in_specs=in_specs, out_specs=out_specs, check_vma=False
    )
```

```python
import functools

import jax
import jax.numpy as jnp
from jax import lax
from jax.experimental import pallas as pl
from jax.experimental.pallas import tpu as pltpu
from jax.sharding import PartitionSpec as P

MESH = pl.DeviceIdType.MESH
f32, bf16 = jnp.float32, jnp.bfloat16

noise_sigma = 0.5
root_coeff = 0.7978845608028654
cubic_coeff = 0.044715

FEAT, HID, TOK, RANK = 1152, 1152, 512, 64
NX, NZ, NT = 4, 8, 16
SHARD = HID // NX
HALF = SHARD // 2
OWN = FEAT // NT
PARTS = ((0, 80), (80, 64), (144, 80), (224, 64))
PLACES = ((0, 80, 144, 224), (720, 800, 432, 512), (864, 1024, 944, 1088), (288, 368, 576, 656))
BLOCKS = (
    (0, 288, ((0, 0, 288),)),
    (288, 288, ((3, 0, 144), (1, 144, 144))),
    (576, 288, ((3, 144, 144), (1, 0, 144))),
    (864, 160, ((2, 0, 80), (2, 144, 80))),
    (1024, 128, ((2, 80, 64), (2, 224, 64))),
)
HALFT = TOK // 2
EARLY = 768
LANES = TOK // 4
MESSAGES = 216
WIDE = 640


def gelu_pair(value):
    inner = root_coeff * (value + cubic_coeff * value * value * value)
    bend = jnp.tanh(inner)
    result = 0.5 * value * (1.0 + bend)
    slope = 0.5 * (1.0 + bend) + 0.5 * value * (1.0 - bend * bend) * root_coeff * (
        1.0 + 3.0 * cubic_coeff * value * value
    )
    return (result, slope)


def dot(left, right):
    return jnp.dot(left, right, preferred_element_type=f32)


def dot_nt(left, right):
    return lax.dot_general(left, right, (((1,), (1,)), ((), ())), preferred_element_type=f32)


def kernel(
    scale_grad,
    tokens_in,
    cotangent_in,
    wgu_in,
    wdn_in,
    ngu_in,
    ndn_in,
    left_t,
    right_n,
    down_left_t,
    down_right_n,
    out_ref,
    grad_ref,
    left_ref,
    right_ref,
    down_left_ref,
    down_right_ref,
    weights,
    noisy,
    noisy_t,
    gathered,
    gathered_c,
    acts,
    left_c,
    right_c,
    right_a,
    lows,
    ranks,
    part,
    core_in,
    y_out,
    y_in,
    back,
    early_out,
    early_grad,
    pieces,
    up_in,
    down_in,
    cross_in,
    y_pieces,
    y_pieces_in,
    y_up_in,
    y_down_in,
    rank_out,
    rank_in,
    draw_in,
    adapters,
    down_rank_out,
    down_rank_in,
    down_draw_in,
    down_adapters,
    lows_core,
    lows_y_out,
    lows_y_in,
    lows_all,
    hid_draw,
    hid_all,
    send_sem,
    recv_sem,
    local_sem,
):
    tensor = lax.axis_index("tensor")
    x = lax.axis_index("draw")
    batch = lax.axis_index("batch")
    yl, z = tensor // NZ, tensor % NZ
    yh, core = batch // 2, batch % 2

    def ring(value, count):
        return (value + count) % count

    x_peers = [{"draw": ring(x + o, NX)} for o in (1, 2, 3)]
    x_right, x_left = x_peers[0], x_peers[2]
    z_up = {"tensor": yl * NZ + ring(z + 1, NZ)}
    z_down = {"tensor": yl * NZ + ring(z - 1, NZ)}
    y_lo = {"tensor": (1 - yl) * NZ + z}
    to_core = {"batch": yh * 2 + 1 - core}
    y_hi = {"batch": (1 - yh) * 2 + core}

    count = [0]
    started = []

    def send(src, dst, where):
        at = count[0]
        count[0] += 1
        assert at < MESSAGES
        copy = pltpu.make_async_remote_copy(
            src_ref=src,
            dst_ref=dst,
            send_sem=send_sem.at[at],
            recv_sem=recv_sem.at[at],
            device_id=where,
            device_id_type=MESH,
        )
        copy.start()
        started.append(copy)
        return copy

    barrier = pltpu.get_barrier_semaphore()
    tensor_peers = [(tensor + o) % NT for o in range(1, NT)]
    partners = [*x_peers, to_core, y_hi, *({"tensor": peer} for peer in tensor_peers)]
    for where in partners:
        pl.semaphore_signal(barrier, inc=1, device_id=where, device_id_type=MESH)
    def side_by_side(value):
        return jnp.concatenate([value[:, :HALFT], value[:, HALFT:]])

    own_tokens, own_cotangent = tokens_in[...].astype(f32), cotangent_in[...].astype(f32)
    gathered[tensor] = side_by_side(own_tokens).astype(bf16)
    gathered_c[tensor] = side_by_side(own_cotangent).astype(bf16)
    pl.semaphore_wait(barrier, len(partners))

    def rows(owner, first=0, size=SHARD):
        return pl.ds(pl.multiple_of(owner * SHARD + first, 16), size)

    owners = [x, ring(x + 1, NX), ring(x + 2, NX), ring(x - 1, NX)]

    def place(owner, piece):
        away = ring(owner - x, NX)
        odd, high = away % 2, away // 2
        right, opposite, left = odd * (1 - high), (1 - odd) * high, odd * high
        first = PLACES[0][piece] * (1 - right - opposite - left) + PLACES[1][piece] * right
        first = first + PLACES[2][piece] * opposite + PLACES[3][piece] * left
        return pl.ds(pl.multiple_of(first, 16), PARTS[piece][1])

    def block(j):
        return pl.ds(BLOCKS[j][0], BLOCKS[j][1])

    y_copy = send(gathered.at[tensor], gathered.at[tensor], y_lo)
    y_copy_c = send(gathered_c.at[tensor], gathered_c.at[tensor], y_lo)
    to_right, to_left = [], []

    def own_shard(half, k):
        source = wgu_in.at[k] if k < 2 else wdn_in
        for flight, turn, where in ((to_right, half, x_right), (to_left, 1 - half, x_left)):
            first = turn * HALF
            flight.append(
                send(source.at[pl.ds(first, HALF)], weights.at[k, rows(x, first, HALF)], where)
            )

    for half in (0, 1):
        for k in (0, 1):
            own_shard(half, k)
    locals_ = [
        pltpu.make_async_copy(ngu_in.at[0], noisy_t.at[0], local_sem.at[1]),
        pltpu.make_async_copy(ngu_in.at[1], noisy_t.at[1], local_sem.at[2]),
        pltpu.make_async_copy(wgu_in.at[0], weights.at[0, rows(x)], local_sem.at[3]),
        pltpu.make_async_copy(wgu_in.at[1], weights.at[1, rows(x)], local_sem.at[4]),
        pltpu.make_async_copy(wdn_in, weights.at[2, rows(x)], local_sem.at[5]),
    ]
    spans = []
    for start, _, parts in BLOCKS:
        for shard, first, size in parts:
            spans.append((start, shard, first, size))
            start += size
    locals_ += [
        pltpu.make_async_copy(
            ndn_in.at[rows(owners[shard], first, size)],
            noisy.at[2, pl.ds(start, size)],
            local_sem.at[6 + at],
        )
        for at, (start, shard, first, size) in enumerate(spans)
    ]
    for copy in locals_:
        copy.start()

    def gather_rings(ref):
        def hop(step, half, up):
            at = half * NZ + (ring(z - step, NZ) if up else ring(z + step, NZ))
            return send(ref.at[at], ref.at[at], z_up if up else z_down)

        flight = {}
        for half in (0, 1):
            for up in (True, False):
                flight[half, up] = hop(0, half, up)
        yield 0
        for step in (1, 2, 3, 4):
            for half in (0, 1):
                for up in (True, False):
                    last = 4 if (half == 0) == up else 3
                    if step > last:
                        continue
                    flight[half, up].wait_recv()
                    if step < last:
                        flight[half, up] = hop(step, half, up)
            yield step

    def flip_noise(first, last):
        def body(strip, _):
            k, at = strip // 9, pl.ds(pl.multiple_of((strip % 9) * 128, 128), 128)
            turned = noisy_t[k, at, :].T
            for i in range(NX):
                for piece, (first, size) in enumerate(PARTS):
                    first += i * SHARD
                    noisy[k, place(i, piece), at] = turned[first : first + size]
            return 0

        lax.fori_loop(first, last, body, 0)

    def flip_back(k_first, k_last, first, last):
        many = last - first

        def body(strip, _):
            k = k_first + strip // many
            at = pl.ds(pl.multiple_of((first + strip % many) * 128, 128), 128)
            noisy_t[k, :, at] = noisy[k, at, :].T
            return 0

        lax.fori_loop(0, (k_last - k_first) * many, body, 0)

    for k in range(3):
        left_c[k] = (left_t[k] if k < 2 else down_right_n[...]).T
        turned = (right_n[k] if k < 2 else down_left_t[...]).T
        for i in range(NX):
            for piece, (first, size) in enumerate(PARTS):
                first += i * SHARD
                right_c[k, place(i, piece), :] = turned[first : first + size]
        right_a[k] = right_c[k].T
    y_copy.wait_recv()
    rings = gather_rings(gathered)
    next(rings)
    locals_[0].wait()
    locals_[1].wait()
    flip_noise(0, 9)
    next(rings)
    flip_noise(9, 18)
    next(rings)
    next(rings)
    next(rings)
    y_copy_c.wait_recv()
    rings = gather_rings(gathered_c)
    next(rings)

    def unpack(source, target):
        def body(m, _):
            one, two = source[2 * m].astype(f32), source[2 * m + 1].astype(f32)
            at = pl.ds(pl.multiple_of(m * 2 * OWN, 16), 2 * OWN)
            acts[target, at, :HALFT] = jnp.concatenate([one[:OWN], two[:OWN]]).astype(bf16)
            acts[target, at, HALFT:] = jnp.concatenate([one[OWN:], two[OWN:]]).astype(bf16)
            return 0

        lax.fori_loop(0, NZ, body, 0)

    x_l, x_r = owners[3], owners[1]
    last = []

    def forward(k, first, size):
        at = weights.at[k, rows(x_l, first, size)]
        last.append(send(at, at, x_right))
        at = weights.at[k, rows(x_r, first + HALF, size)]
        last.append(send(at, at, x_left))

    def spread(j, k_first, k_last):
        start, size, parts = BLOCKS[j]

        def body(k, _):
            at = start
            for shard, first, count in parts:
                here = pl.ds(at, count)
                noisy[k, here, :] = (
                    weights[k, rows(owners[shard], first, count), :].astype(f32)
                    * (1.0 + noise_sigma * noisy[k, here, :].astype(f32))
                ).astype(bf16)
                at += count
            total = dot(noisy[k, block(j), :], acts[k // 2])
            total = total + dot(right_c[k, block(j), :], lows[k])
            for b in range(4):
                part[b % 2, b // 2, k, block(j), :] = total[:, b * LANES : (b + 1) * LANES].astype(
                    bf16
                )
            return 0

        lax.fori_loop(k_first, k_last, body, 0)
        ks = pl.ds(k_first, k_last - k_first)
        return send(part.at[1 - core, :, ks, block(j)], core_in.at[:, ks, block(j)], to_core)

    def cores(j, k_first, k_last, copy):
        copy.wait_recv()
        at, ks = block(j), pl.ds(k_first, k_last - k_first)
        for half in (0, 1):
            for k in range(k_first, k_last):
                y_out[half, k, at, :] = (
                    part[core, half, k, at, :].astype(f32) + core_in[half, k, at, :].astype(f32)
                ).astype(bf16)
        return send(y_out.at[:, ks, at], y_in.at[:, ks, at], y_hi)

    def whole(half, k, at):
        return y_out[half, k, at, :].astype(f32) + y_in[half, k, at, :].astype(f32)

    def bend(j, copy):
        copy.wait_recv()
        at = block(j)
        for half in (0, 1):
            active, _ = gelu_pair(whole(half, 0, at))
            back[core, half, 2, at, :] = (active * whole(half, 1, at)).astype(bf16)
        mine = back.at[core, :, 2, at]
        return send(mine, mine, to_core)

    def bend_grad(j, copy):
        copy.wait_recv()
        at = block(j)
        for half in (0, 1):
            active, slope = gelu_pair(whole(half, 0, at))
            grad = whole(half, 2, at)
            back[core, half, 0, at, :] = (grad * whole(half, 1, at) * slope).astype(bf16)
            back[core, half, 1, at, :] = (grad * active).astype(bf16)
        mine = back.at[core, :, pl.ds(0, 2), at]
        return send(mine, mine, to_core)

    def all_tokens(k, first=0, last=HID):
        return jnp.concatenate([back[b % 2, b // 2, k, first:last, :] for b in range(4)], axis=1)

    def finish(copy):
        copy.wait_recv()

    def early_outputs(m, _):
        at = pl.ds(pl.multiple_of(m * SHARD, 16), SHARD)
        early_out[at, :] = dot(noisy_t[2, at, :EARLY], all_tokens(2, 0, EARLY))
        return 0

    def early_grads(m, _):
        at = pl.ds(pl.multiple_of(m * SHARD, 16), SHARD)
        early_grad[at, :] = dot(noisy_t[0, at, :EARLY], all_tokens(0, 0, EARLY)) + dot(
            noisy_t[1, at, :EARLY], all_tokens(1, 0, EARLY)
        )
        return 0

    for k in (0, 1):
        to_right[k].wait_recv()
        to_left[k].wait_recv()
    for k in (0, 1):
        forward(k, 0, 80)
    for k in (0, 1):
        forward(k, 80, 64)
    own_shard(0, 2)
    own_shard(1, 2)
    unpack(gathered, 0)
    lows[0] = dot(left_t[0], acts[0]).astype(bf16)
    lows[1] = dot(left_t[1], acts[0]).astype(bf16)
    for copy in locals_[2:]:
        copy.wait()
    g0 = spread(0, 0, 2)
    g1 = spread(1, 0, 2)
    next(rings)
    g0 = cores(0, 0, 2, g0)
    g1 = cores(1, 0, 2, g1)
    next(rings)
    for k in (2, 3):
        to_right[k].wait_recv()
        to_left[k].wait_recv()
    g2 = spread(2, 0, 2)
    next(rings)
    g2 = cores(2, 0, 2, g2)
    next(rings)
    unpack(gathered_c, 1)
    lows[2] = dot(down_right_n[...], acts[1]).astype(bf16)
    def select(shape, test):
        row, column = (lax.broadcasted_iota(jnp.int32, shape, axis) for axis in (0, 1))
        return jnp.where(test(row, column), 1.0, 0.0).astype(bf16)

    def over_draws(ref):
        total = (ref[0].astype(f32) + ref[1].astype(f32)) + (ref[2].astype(f32) + ref[3].astype(f32))
        return (scale_grad * total).astype(bf16)

    def sum_units(out, box):
        total = out[tensor].astype(f32)
        for o in range(NT - 1):
            total = total + box[o].astype(f32)
        return total

    z_order = (1, 7, 2, 6, 3, 5, 4)

    def spread_adapters(ref):
        mine = ref.at[tensor]
        near = [send(mine, mine, {"tensor": yl * NZ + ring(z + o, NZ)}) for o in z_order]
        return near, [send(mine, mine, y_lo)]

    def forward_adapters(ref, near, far, these):
        for at in these:
            near[at].wait_recv()
            there = ref.at[yl * NZ + ring(z - z_order[at], NZ)]
            far.append(send(there, there, y_lo))

    def down_ranks():
        chosen = select(
            (16 * NT, RANK),
            lambda row, column: jnp.logical_and(row % 16 < 4, column == row // 16 * 4 + row % 16),
        )
        boxed = dot(chosen, ranks[2 * RANK :, :]).astype(bf16)
        for unit in range(NT):
            down_rank_out[unit] = boxed[16 * unit : 16 * (unit + 1)]
        return [
            send(down_rank_out.at[peer], down_rank_in.at[o], {"tensor": peer})
            for o, peer in enumerate(tensor_peers)
        ]

    def down_draws(copies):
        for copy in copies:
            copy.wait_recv()
        total = sum_units(down_rank_out, down_rank_in).astype(bf16)
        rows_f = dot_nt(total, acts[1]).astype(bf16)
        third, folded = FEAT // 3, None
        for q in range(3):
            chosen = select(
                (16, 16),
                lambda row, column: jnp.logical_and(row == column + 4 * q, column < 4),
            )
            piece = dot(chosen, rows_f[:, q * third : (q + 1) * third])
            folded = piece if folded is None else folded + piece
        down_draw_in[x] = folded.astype(bf16)
        mine = down_draw_in.at[x]
        return [send(mine, mine, where) for where in x_peers]

    def down_spread(copies):
        for copy in copies:
            copy.wait_recv()
        down_adapters[tensor] = over_draws(down_draw_in)
        return spread_adapters(down_adapters)

    low_sum = send(lows, lows_core, to_core)
    d0 = spread(0, 2, 3)
    g0 = bend(0, g0)
    low_sum.wait_recv()
    lows_y_out[...] = (lows[...].astype(f32) + lows_core[...].astype(f32)).astype(bf16)
    low_sum = send(lows_y_out, lows_y_in, y_hi)
    d0 = cores(0, 2, 3, d0)
    for copy in last[:4]:
        copy.wait_recv()
    g3 = spread(3, 0, 2)
    flip_back(0, 2, 0, 6)
    g3 = cores(3, 0, 2, g3)
    g1 = bend(1, g1)
    finish(g0)
    low_sum.wait_recv()
    lows_all[...] = (lows_y_out[...].astype(f32) + lows_y_in[...].astype(f32)).astype(bf16)
    for copy in last[4:8]:
        copy.wait_recv()
    g4 = spread(4, 0, 2)
    finish(g1)
    g4 = cores(4, 0, 2, g4)
    flip_back(0, 2, 6, 9)
    g2 = bend(2, g2)
    to_right[4].wait_recv()
    to_left[4].wait_recv()
    forward(2, 0, 80)
    forward(2, 80, 64)
    d1 = spread(1, 2, 3)
    d0 = bend_grad(0, d0)
    finish(g2)
    d1 = cores(1, 2, 3, d1)
    g3 = bend(3, g3)
    finish(d0)
    finish(g3)
    to_right[5].wait_recv()
    to_left[5].wait_recv()
    d2 = spread(2, 2, 3)
    g4 = bend(4, g4)
    d2 = cores(2, 2, 3, d2)
    flip_back(2, 3, 0, 6)
    lax.fori_loop(0, 4, early_outputs, 0)
    finish(g4)
    for copy in last[8:10]:
        copy.wait_recv()
    d3 = spread(3, 2, 3)
    d1 = bend_grad(1, d1)
    ranks[pl.ds(2 * RANK, RANK), :] = dot(right_a[2], all_tokens(2)).astype(bf16)
    down_sums = down_ranks()
    d3 = cores(3, 2, 3, d3)
    for copy in last[10:]:
        copy.wait_recv()
    d4 = spread(4, 2, 3)
    flip_back(2, 3, 6, 9)
    d4 = cores(4, 2, 3, d4)

    def outputs(half, group):
        m = half * 2 + group
        at = pl.ds(pl.multiple_of(m * SHARD, 16), SHARD)
        out = early_out[at, :] + dot(noisy_t[2, at, EARLY:], all_tokens(2, EARLY))
        out = out + dot(left_c[2, at, :], ranks[128:192, :])
        for i in range(4):
            pieces[4 * m + i] = side_by_side(out[i * OWN : (i + 1) * OWN]).astype(bf16)
        return group

    def pass_on(step, half, up, copy):
        target = half * NZ + (ring(z + 4 - step, NZ) if up else ring(z - 4 + step, NZ))
        box = (up_in if up else down_in).at[step, half]
        if copy is not None:
            copy.wait_recv()
            came = (up_in if up else down_in)[step - 1, half]
            pieces[target] = (pieces[target].astype(f32) + came.astype(f32)).astype(bf16)
        return send(pieces.at[target], box, z_up if up else z_down)

    flight = {}

    def go(step, half, up):
        flight[half, up] = pass_on(step, half, up, flight.get((half, up)))

    lax.fori_loop(0, 2, outputs, 1 - z // 4)
    go(0, 0, True)
    go(0, 1, False)
    lax.fori_loop(0, 2, outputs, z // 4)
    go(1, 1, True)
    go(1, 0, False)
    d2 = bend_grad(2, d2)
    down_sums = down_draws(down_sums)
    finish(d1)
    finish(d2)
    d3 = bend_grad(3, d3)
    go(1, 0, True)
    go(1, 1, False)
    lax.fori_loop(0, 4, early_grads, 0)
    d4 = bend_grad(4, d4)
    down_near, down_far = down_spread(down_sums)
    finish(d3)
    finish(d4)

    for k in (0, 1):
        ranks[pl.ds(k * RANK, RANK), :] = dot(right_a[k], all_tokens(k)).astype(bf16)
    halves = []
    for half in (0, 1):
        chosen = select(
            (8 * NT, 2 * RANK),
            lambda row, column: column == row % 8 // 4 * RANK + row // 8 * 4 + row % 4,
        )
        halves.append(dot(chosen, ranks[: 2 * RANK, half * HALFT : (half + 1) * HALFT]))
    for unit in range(NT):
        at = slice(8 * unit, 8 * (unit + 1))
        rank_out[unit] = jnp.concatenate([halves[0][at], halves[1][at]]).astype(bf16)
    r1 = [
        send(rank_out.at[peer], rank_in.at[o], {"tensor": peer})
        for o, peer in enumerate(tensor_peers)
    ]

    quarter = core * 2 + yh
    for piece, (first, size) in enumerate(PARTS):
        at = place(quarter, piece)
        turned = [
            dot_nt(
                jnp.concatenate([back[b % 2, b // 2, k, at, :] for b in range(4)], axis=1),
                lows_all[k],
            )
            for k in (0, 1, 2, 2)
        ]
        hid_draw[x, pl.ds(first, size), :] = jnp.concatenate(turned, axis=1).astype(bf16)
    h3 = [send(hid_draw.at[x], hid_draw.at[x], where) for where in x_peers]
    own_rows = pl.ds(pl.multiple_of(quarter * SHARD, 16), SHARD)
    far_rows = pl.ds(pl.multiple_of((core * 2 + 1 - yh) * SHARD, 16), SHARD)

    def grads(half, group):
        m = half * 2 + group
        at = pl.ds(pl.multiple_of(m * SHARD, 16), SHARD)
        grad = early_grad[at, :] + dot(noisy_t[0, at, EARLY:], all_tokens(0, EARLY))
        grad = grad + dot(noisy_t[1, at, EARLY:], all_tokens(1, EARLY))
        grad = grad + dot(left_c[0, at, :], ranks[0:64, :]) + dot(left_c[1, at, :], ranks[64:128, :])
        for i in range(4):
            y_pieces[4 * m + i] = side_by_side(grad[i * OWN : (i + 1) * OWN]).astype(bf16)
        return group

    def cross_y(target):
        at = (1 - yl) * NZ + ring(target, NZ)
        return send(y_pieces.at[at], y_pieces_in.at[ring(target, NZ)], y_lo)

    def y_pass(step, up, copy, arrived):
        target = ring(z + 4 - step, NZ) if up else ring(z - 3 + step, NZ)
        box = y_up_in if up else y_down_in
        arrived.wait_recv()
        total = y_pieces[yl * NZ + target].astype(f32) + y_pieces_in[target].astype(f32)
        if copy is not None:
            copy.wait_recv()
            total = total + box[step - 1].astype(f32)
        y_pieces[yl * NZ + target] = total.astype(bf16)
        return send(y_pieces.at[yl * NZ + target], box.at[step], z_up if up else z_down)

    lax.fori_loop(0, 2, grads, 1 - z // 4)
    crossed = {4: cross_y(z + 4)}
    go(2, 1, True)
    go(2, 0, False)
    lax.fori_loop(0, 2, grads, z // 4)
    for away in (3, -3, 2, -2, 1, -1, 0):
        crossed[away] = cross_y(z + away)
    go(2, 0, True)
    go(2, 1, False)
    for copy in r1:
        copy.wait_recv()
    total = sum_units(rank_out, rank_in)
    total = jnp.concatenate([total[:8], total[8:]], axis=1).astype(bf16)
    total = jnp.concatenate([total.astype(f32)] * 2).astype(bf16)
    rows_f = dot_nt(total, acts[0])
    rest = jnp.concatenate([rows_f[8:, WIDE:], rows_f[8:, : 2 * WIDE - FEAT]], axis=1)
    draw_in[x] = jnp.concatenate([rows_f[:8, :WIDE], rest]).astype(bf16)
    d1 = [send(draw_in.at[x], draw_in.at[x], where) for where in x_peers]
    y_up = y_pass(0, True, None, crossed[4])
    go(3, 1, True)
    go(3, 0, False)
    y_down = y_pass(0, False, None, crossed[-3])
    go(3, 0, True)
    go(3, 1, False)
    for copy in d1:
        copy.wait_recv()
    adapters[tensor] = over_draws(draw_in)
    near, far = spread_adapters(adapters)
    forward_adapters(down_adapters, down_near, down_far, range(7))
    y_up = y_pass(1, True, y_up, crossed[3])
    y_down = y_pass(1, False, y_down, crossed[-2])

    for copy in h3:
        copy.wait_recv()
    hid_all[own_rows, :] = over_draws(hid_draw)
    h4 = [
        send(hid_all.at[own_rows], hid_all.at[own_rows], y_hi),
        send(hid_all.at[own_rows], hid_all.at[own_rows], to_core),
    ]

    for copy in flight.values():
        copy.wait_recv()

    def over_z(half):
        return (
            pieces[half * NZ + z].astype(f32)
            + up_in[3, half].astype(f32)
            + down_in[3, half].astype(f32)
        )

    y_piece = (1 - yl) * NZ + z
    pieces[y_piece] = over_z(1 - yl).astype(bf16)
    cross = send(pieces.at[y_piece], cross_in, y_lo)
    y_up = y_pass(2, True, y_up, crossed[2])
    y_down = y_pass(2, False, y_down, crossed[-1])
    y_up = y_pass(3, True, y_up, crossed[1])

    forward_adapters(adapters, near, far, range(4))
    h4[0].wait_recv()
    h4.append(send(hid_all.at[far_rows], hid_all.at[far_rows], to_core))
    cross.wait_recv()
    first = over_z(yl) + cross_in[...].astype(f32)
    out_ref[:, :HALFT] = first[:OWN].astype(bf16)
    out_ref[:, HALFT:] = first[OWN:].astype(bf16)
    forward_adapters(adapters, near, far, range(4, 7))
    y_up.wait_recv()
    y_down.wait_recv()
    crossed[0].wait_recv()
    second = (
        (y_pieces[yl * NZ + z].astype(f32) + y_pieces_in[z].astype(f32))
        + y_up_in[3].astype(f32)
        + y_down_in[2].astype(f32)
    )
    grad_ref[:, :HALFT] = second[:OWN].astype(bf16)
    grad_ref[:, HALFT:] = second[OWN:].astype(bf16)
    h4[1].wait_recv()
    h4[2].wait_recv()
    turned = hid_all[...].astype(f32).T
    right_ref[0] = turned[:RANK].astype(bf16)
    right_ref[1] = turned[RANK : 2 * RANK].astype(bf16)
    down_left_ref[...] = turned[2 * RANK : 3 * RANK].astype(bf16)
    for copy in down_far:
        copy.wait_recv()
    stacked = jnp.concatenate([down_adapters[unit] for unit in range(NT)])
    for q in range(3):
        chosen = select(
            (RANK, 16 * NT), lambda row, column: column == row // 4 * 16 + row % 4 + 4 * q
        )
        third = slice(q * FEAT // 3, (q + 1) * FEAT // 3)
        down_right_ref[:, third] = dot(chosen, stacked).astype(bf16)
    for copy in far:
        copy.wait_recv()
    stacked = jnp.concatenate([adapters[unit] for unit in range(NT)])
    for q in (0, 1):
        chosen = select(
            (2 * RANK, 16 * NT),
            lambda row, column: column
            == row % RANK // 4 * 16 + row // RANK * 4 + row % 4 + 8 * q,
        )
        wide = WIDE if q == 0 else FEAT - WIDE
        turned = dot(chosen, stacked[:, :wide]).astype(bf16)
        at = slice(q * WIDE, q * WIDE + wide)
        left_ref[0, :, at] = turned[:RANK]
        left_ref[1, :, at] = turned[RANK:]
    for copy in started:
        copy.wait_send()


def hand_over(*refs):
    for source, target in zip(refs[:6], refs[6:]):
        target[...] = source[...]


def on_device(
    tokens,
    cotangent,
    gate_up_weight,
    down_weight,
    gate_up_noise,
    down_noise,
    gate_up_left,
    gate_up_right,
    down_left,
    down_right,
):
    scale_grad = (NX * TOK) ** (-0.5)
    vmem, anywhere = pl.BlockSpec(memory_space=pltpu.VMEM), pl.BlockSpec(memory_space=pl.ANY)
    scratch = [
        pltpu.VMEM((3, HID, FEAT), bf16),
        pltpu.VMEM((3, HID, FEAT), bf16),
        pltpu.VMEM((3, FEAT, HID), bf16),
        pltpu.VMEM((NT, 2 * OWN, HALFT), bf16),
        pltpu.VMEM((NT, 2 * OWN, HALFT), bf16),
        pltpu.VMEM((2, FEAT, TOK), bf16),
        pltpu.VMEM((3, FEAT, RANK), bf16),
        pltpu.VMEM((3, HID, RANK), bf16),
        pltpu.VMEM((3, RANK, HID), bf16),
        pltpu.VMEM((3, RANK, TOK), bf16),
        pltpu.VMEM((3 * RANK, TOK), bf16),
        pltpu.VMEM((2, 2, 3, HID, LANES), bf16),
        pltpu.VMEM((2, 3, HID, LANES), bf16),
        pltpu.VMEM((2, 3, HID, LANES), bf16),
        pltpu.VMEM((2, 3, HID, LANES), bf16),
        pltpu.VMEM((2, 2, 3, HID, LANES), bf16),
        pltpu.VMEM((FEAT, TOK), f32),
        pltpu.VMEM((FEAT, TOK), f32),
        pltpu.VMEM((NT, 2 * OWN, HALFT), bf16),
        pltpu.VMEM((4, 2, 2 * OWN, HALFT), bf16),
        pltpu.VMEM((4, 2, 2 * OWN, HALFT), bf16),
        pltpu.VMEM((2 * OWN, HALFT), bf16),
        pltpu.VMEM((NT, 2 * OWN, HALFT), bf16),
        pltpu.VMEM((NZ, 2 * OWN, HALFT), bf16),
        pltpu.VMEM((4, 2 * OWN, HALFT), bf16),
        pltpu.VMEM((3, 2 * OWN, HALFT), bf16),
        pltpu.VMEM((NT, 16, HALFT), bf16),
        pltpu.VMEM((NT, 16, HALFT), bf16),
        pltpu.VMEM((NX, 16, WIDE), bf16),
        pltpu.VMEM((NT, 16, WIDE), bf16),
        pltpu.VMEM((NT, 16, TOK), bf16),
        pltpu.VMEM((NT, 16, TOK), bf16),
        pltpu.VMEM((NX, 16, FEAT // 3), bf16),
        pltpu.VMEM((NT, 16, FEAT // 3), bf16),
        pltpu.VMEM((3, RANK, TOK), bf16),
        pltpu.VMEM((3, RANK, TOK), bf16),
        pltpu.VMEM((3, RANK, TOK), bf16),
        pltpu.VMEM((3, RANK, TOK), bf16),
        pltpu.VMEM((NX, SHARD, 4 * RANK), bf16),
        pltpu.VMEM((HID, 4 * RANK), bf16),
        pltpu.SemaphoreType.DMA((MESSAGES,)),
        pltpu.SemaphoreType.DMA((MESSAGES,)),
        pltpu.SemaphoreType.DMA((16,)),
    ]
    shapes = [
        (OWN, TOK),
        (OWN, TOK),
        (2, RANK, FEAT),
        (2, RANK, HID),
        (RANK, HID),
        (RANK, FEAT),
    ]
    shapes = tuple(jax.ShapeDtypeStruct(shape, bf16) for shape in shapes)
    results = pl.pallas_call(
        functools.partial(kernel, scale_grad),
        out_shape=shapes,
        in_specs=[vmem] * 2 + [anywhere] * 4 + [vmem] * 4,
        out_specs=(vmem,) * 6,
        scratch_shapes=scratch,
        compiler_params=pltpu.CompilerParams(
            collective_id=0, has_side_effects=True, vmem_limit_bytes=62 * 2**20
        ),
    )(
        tokens[0].T,
        cotangent[0].T,
        jnp.swapaxes(gate_up_weight, 1, 2),
        down_weight,
        gate_up_noise[0],
        down_noise[0],
        jnp.swapaxes(gate_up_left, 1, 2),
        gate_up_right,
        down_left.T,
        down_right,
    )
    out, grad, left, right, down_left_grad, down_right_grad = pl.pallas_call(
        hand_over, out_shape=shapes, in_specs=[vmem] * 6, out_specs=(vmem,) * 6
    )(*results)
    return (
        out.T[None],
        grad.T[None],
        jnp.swapaxes(left, 1, 2),
        right,
        down_left_grad.T,
        down_right_grad,
    )


def solution(mesh):
    in_specs = (
        P("draw", None, ("batch", "tensor")),
        P("draw", None, ("batch", "tensor")),
        P(None, "batch", ("tensor", "draw")),
        P(("tensor", "draw"), "batch"),
        P("draw", None, "batch", "tensor"),
        P("draw", "tensor", "batch"),
        P(None, "batch", None),
        P(None, None, "tensor"),
        P("tensor", None),
        P(None, "batch"),
    )
    out_specs = (
        P("draw", None, ("batch", "tensor")),
        P("draw", None, ("batch", "tensor")),
        P(None, "batch", None),
        P(None, None, "tensor"),
        P("tensor", None),
        P(None, "batch"),
    )
    return jax.shard_map(
        on_device, mesh=mesh, in_specs=in_specs, out_specs=out_specs, check_vma=False
    )
```

```python
import functools

import jax
import jax.numpy as jnp
from jax import lax
from jax.experimental import pallas as pl
from jax.experimental.pallas import tpu as pltpu
from jax.sharding import PartitionSpec as P

MESH = pl.DeviceIdType.MESH
f32, bf16 = jnp.float32, jnp.bfloat16

noise_sigma = 0.5
root_coeff = 0.7978845608028654
cubic_coeff = 0.044715

FEAT, HID, TOK, RANK = 1152, 1152, 512, 64
NX, NZ, NT = 4, 8, 16
SHARD = HID // NX
HALF = SHARD // 2
OWN = FEAT // NT
PARTS = ((0, 80), (80, 64), (144, 80), (224, 64))
PLACES = ((0, 80, 144, 224), (720, 800, 432, 512), (864, 1024, 944, 1088), (288, 368, 576, 656))
BLOCKS = (
    (0, 288, ((0, 0, 288),)),
    (288, 288, ((3, 0, 144), (1, 144, 144))),
    (576, 288, ((3, 144, 144), (1, 0, 144))),
    (864, 160, ((2, 0, 80), (2, 144, 80))),
    (1024, 128, ((2, 80, 64), (2, 224, 64))),
)
HALFT = TOK // 2
EARLY = 768
LANES = TOK // 4
MESSAGES = 216
WIDE = 640


def gelu_pair(value):
    inner = root_coeff * (value + cubic_coeff * value * value * value)
    bend = jnp.tanh(inner)
    result = 0.5 * value * (1.0 + bend)
    slope = 0.5 * (1.0 + bend) + 0.5 * value * (1.0 - bend * bend) * root_coeff * (
        1.0 + 3.0 * cubic_coeff * value * value
    )
    return (result, slope)


def dot(left, right):
    return jnp.dot(left, right, preferred_element_type=f32)


def dot_nt(left, right):
    return lax.dot_general(left, right, (((1,), (1,)), ((), ())), preferred_element_type=f32)


def kernel(
    scale_grad,
    tokens_in,
    cotangent_in,
    wgu_in,
    wdn_in,
    ngu_in,
    ndn_in,
    left_t,
    right_n,
    down_left_t,
    down_right_n,
    out_ref,
    grad_ref,
    left_ref,
    right_ref,
    down_left_ref,
    down_right_ref,
    weights,
    noisy,
    noisy_t,
    gathered,
    gathered_c,
    acts,
    left_c,
    right_c,
    right_a,
    lows,
    ranks,
    part,
    core_in,
    y_out,
    y_in,
    back,
    early_out,
    early_grad,
    pieces,
    up_in,
    down_in,
    cross_in,
    y_pieces,
    y_pieces_in,
    y_up_in,
    y_down_in,
    rank_out,
    rank_in,
    draw_in,
    adapters,
    down_rank_out,
    down_rank_in,
    down_draw_in,
    down_adapters,
    lows_core,
    lows_y_out,
    lows_y_in,
    lows_all,
    hid_draw,
    hid_all,
    send_sem,
    recv_sem,
    local_sem,
):
    tensor = lax.axis_index("tensor")
    x = lax.axis_index("draw")
    batch = lax.axis_index("batch")
    yl, z = tensor // NZ, tensor % NZ
    yh, core = batch // 2, batch % 2

    def ring(value, count):
        return (value + count) % count

    x_peers = [{"draw": ring(x + o, NX)} for o in (1, 2, 3)]
    x_right, x_left = x_peers[0], x_peers[2]
    z_up = {"tensor": yl * NZ + ring(z + 1, NZ)}
    z_down = {"tensor": yl * NZ + ring(z - 1, NZ)}
    y_lo = {"tensor": (1 - yl) * NZ + z}
    to_core = {"batch": yh * 2 + 1 - core}
    y_hi = {"batch": (1 - yh) * 2 + core}

    count = [0]
    started = []

    def send(src, dst, where):
        at = count[0]
        count[0] += 1
        assert at < MESSAGES
        copy = pltpu.make_async_remote_copy(
            src_ref=src,
            dst_ref=dst,
            send_sem=send_sem.at[at],
            recv_sem=recv_sem.at[at],
            device_id=where,
            device_id_type=MESH,
        )
        copy.start()
        started.append(copy)
        return copy

    barrier = pltpu.get_barrier_semaphore()
    tensor_peers = [(tensor + o) % NT for o in range(1, NT)]
    partners = [*x_peers, to_core, y_hi, *({"tensor": peer} for peer in tensor_peers)]
    for where in partners:
        pl.semaphore_signal(barrier, inc=1, device_id=where, device_id_type=MESH)
    def side_by_side(value):
        return jnp.concatenate([value[:, :HALFT], value[:, HALFT:]])

    own_tokens, own_cotangent = tokens_in[...].astype(f32), cotangent_in[...].astype(f32)
    gathered[tensor] = side_by_side(own_tokens).astype(bf16)
    gathered_c[tensor] = side_by_side(own_cotangent).astype(bf16)
    pl.semaphore_wait(barrier, len(partners))

    def rows(owner, first=0, size=SHARD):
        return pl.ds(pl.multiple_of(owner * SHARD + first, 16), size)

    owners = [x, ring(x + 1, NX), ring(x + 2, NX), ring(x - 1, NX)]

    def place(owner, piece):
        away = ring(owner - x, NX)
        odd, high = away % 2, away // 2
        right, opposite, left = odd * (1 - high), (1 - odd) * high, odd * high
        first = PLACES[0][piece] * (1 - right - opposite - left) + PLACES[1][piece] * right
        first = first + PLACES[2][piece] * opposite + PLACES[3][piece] * left
        return pl.ds(pl.multiple_of(first, 16), PARTS[piece][1])

    def block(j):
        return pl.ds(BLOCKS[j][0], BLOCKS[j][1])

    y_copy = send(gathered.at[tensor], gathered.at[tensor], y_lo)
    y_copy_c = send(gathered_c.at[tensor], gathered_c.at[tensor], y_lo)
    to_right, to_left = [], []

    def own_shard(half, k):
        source = wgu_in.at[k] if k < 2 else wdn_in
        for flight, turn, where in ((to_right, half, x_right), (to_left, 1 - half, x_left)):
            first = turn * HALF
            flight.append(
                send(source.at[pl.ds(first, HALF)], weights.at[k, rows(x, first, HALF)], where)
            )

    for half in (0, 1):
        for k in (0, 1):
            own_shard(half, k)
    locals_ = [
        pltpu.make_async_copy(ngu_in.at[0], noisy_t.at[0], local_sem.at[1]),
        pltpu.make_async_copy(ngu_in.at[1], noisy_t.at[1], local_sem.at[2]),
        pltpu.make_async_copy(wgu_in.at[0], weights.at[0, rows(x)], local_sem.at[3]),
        pltpu.make_async_copy(wgu_in.at[1], weights.at[1, rows(x)], local_sem.at[4]),
        pltpu.make_async_copy(wdn_in, weights.at[2, rows(x)], local_sem.at[5]),
    ]
    spans = []
    for start, _, parts in BLOCKS:
        for shard, first, size in parts:
            spans.append((start, shard, first, size))
            start += size
    locals_ += [
        pltpu.make_async_copy(
            ndn_in.at[rows(owners[shard], first, size)],
            noisy.at[2, pl.ds(start, size)],
            local_sem.at[6 + at],
        )
        for at, (start, shard, first, size) in enumerate(spans)
    ]
    for copy in locals_:
        copy.start()

    def gather_rings(ref):
        def hop(step, half, up):
            at = half * NZ + (ring(z - step, NZ) if up else ring(z + step, NZ))
            return send(ref.at[at], ref.at[at], z_up if up else z_down)

        flight = {}
        for half in (0, 1):
            for up in (True, False):
                flight[half, up] = hop(0, half, up)
        yield 0
        for step in (1, 2, 3, 4):
            for half in (0, 1):
                for up in (True, False):
                    last = 4 if (half == 0) == up else 3
                    if step > last:
                        continue
                    flight[half, up].wait_recv()
                    if step < last:
                        flight[half, up] = hop(step, half, up)
            yield step

    def flip_noise(first, last):
        def body(strip, _):
            k, at = strip // 9, pl.ds(pl.multiple_of((strip % 9) * 128, 128), 128)
            turned = noisy_t[k, at, :].T
            for i in range(NX):
                for piece, (first, size) in enumerate(PARTS):
                    first += i * SHARD
                    noisy[k, place(i, piece), at] = turned[first : first + size]
            return 0

        lax.fori_loop(first, last, body, 0)

    def flip_back(k_first, k_last, first, last):
        many = last - first

        def body(strip, _):
            k = k_first + strip // many
            at = pl.ds(pl.multiple_of((first + strip % many) * 128, 128), 128)
            noisy_t[k, :, at] = noisy[k, at, :].T
            return 0

        lax.fori_loop(0, (k_last - k_first) * many, body, 0)

    for k in range(3):
        left_c[k] = (left_t[k] if k < 2 else down_right_n[...]).T
        turned = (right_n[k] if k < 2 else down_left_t[...]).T
        for i in range(NX):
            for piece, (first, size) in enumerate(PARTS):
                first += i * SHARD
                right_c[k, place(i, piece), :] = turned[first : first + size]
        right_a[k] = right_c[k].T
    y_copy.wait_recv()
    rings = gather_rings(gathered)
    next(rings)
    locals_[0].wait()
    locals_[1].wait()
    flip_noise(0, 9)
    next(rings)
    flip_noise(9, 18)
    next(rings)
    next(rings)
    next(rings)
    y_copy_c.wait_recv()
    rings = gather_rings(gathered_c)
    next(rings)

    def unpack(source, target):
        def body(m, _):
            one, two = source[2 * m].astype(f32), source[2 * m + 1].astype(f32)
            at = pl.ds(pl.multiple_of(m * 2 * OWN, 16), 2 * OWN)
            acts[target, at, :HALFT] = jnp.concatenate([one[:OWN], two[:OWN]]).astype(bf16)
            acts[target, at, HALFT:] = jnp.concatenate([one[OWN:], two[OWN:]]).astype(bf16)
            return 0

        lax.fori_loop(0, NZ, body, 0)

    x_l, x_r = owners[3], owners[1]
    last = []

    def forward(k, first, size):
        at = weights.at[k, rows(x_l, first, size)]
        last.append(send(at, at, x_right))
        at = weights.at[k, rows(x_r, first + HALF, size)]
        last.append(send(at, at, x_left))

    def spread(j, k_first, k_last):
        start, size, parts = BLOCKS[j]

        def body(k, _):
            at = start
            for shard, first, count in parts:
                here = pl.ds(at, count)
                noisy[k, here, :] = (
                    weights[k, rows(owners[shard], first, count), :].astype(f32)
                    * (1.0 + noise_sigma * noisy[k, here, :].astype(f32))
                ).astype(bf16)
                at += count
            total = dot(noisy[k, block(j), :], acts[k // 2])
            total = total + dot(right_c[k, block(j), :], lows[k])
            for b in range(4):
                part[b % 2, b // 2, k, block(j), :] = total[:, b * LANES : (b + 1) * LANES].astype(
                    bf16
                )
            return 0

        lax.fori_loop(k_first, k_last, body, 0)
        ks = pl.ds(k_first, k_last - k_first)
        return send(part.at[1 - core, :, ks, block(j)], core_in.at[:, ks, block(j)], to_core)

    def cores(j, k_first, k_last, copy):
        copy.wait_recv()
        at, ks = block(j), pl.ds(k_first, k_last - k_first)
        for half in (0, 1):
            for k in range(k_first, k_last):
                y_out[half, k, at, :] = (
                    part[core, half, k, at, :].astype(f32) + core_in[half, k, at, :].astype(f32)
                ).astype(bf16)
        return send(y_out.at[:, ks, at], y_in.at[:, ks, at], y_hi)

    def whole(half, k, at):
        return y_out[half, k, at, :].astype(f32) + y_in[half, k, at, :].astype(f32)

    def bend(j, copy):
        copy.wait_recv()
        at = block(j)
        for half in (0, 1):
            active, _ = gelu_pair(whole(half, 0, at))
            back[core, half, 2, at, :] = (active * whole(half, 1, at)).astype(bf16)
        mine = back.at[core, :, 2, at]
        return send(mine, mine, to_core)

    def bend_grad(j, copy):
        copy.wait_recv()
        at = block(j)
        for half in (0, 1):
            active, slope = gelu_pair(whole(half, 0, at))
            grad = whole(half, 2, at)
            back[core, half, 0, at, :] = (grad * whole(half, 1, at) * slope).astype(bf16)
            back[core, half, 1, at, :] = (grad * active).astype(bf16)
        mine = back.at[core, :, pl.ds(0, 2), at]
        return send(mine, mine, to_core)

    def all_tokens(k, first=0, last=HID):
        return jnp.concatenate([back[b % 2, b // 2, k, first:last, :] for b in range(4)], axis=1)

    def finish(copy):
        copy.wait_recv()

    def early_outputs(m, _):
        at = pl.ds(pl.multiple_of(m * SHARD, 16), SHARD)
        early_out[at, :] = dot(noisy_t[2, at, :EARLY], all_tokens(2, 0, EARLY))
        return 0

    def early_grads(m, _):
        at = pl.ds(pl.multiple_of(m * SHARD, 16), SHARD)
        early_grad[at, :] = dot(noisy_t[0, at, :EARLY], all_tokens(0, 0, EARLY)) + dot(
            noisy_t[1, at, :EARLY], all_tokens(1, 0, EARLY)
        )
        return 0

    for k in (0, 1):
        to_right[k].wait_recv()
        to_left[k].wait_recv()
    for k in (0, 1):
        forward(k, 0, 80)
    for k in (0, 1):
        forward(k, 80, 64)
    own_shard(0, 2)
    own_shard(1, 2)
    unpack(gathered, 0)
    lows[0] = dot(left_t[0], acts[0]).astype(bf16)
    lows[1] = dot(left_t[1], acts[0]).astype(bf16)
    for copy in locals_[2:]:
        copy.wait()
    g0 = spread(0, 0, 2)
    g1 = spread(1, 0, 2)
    next(rings)
    g0 = cores(0, 0, 2, g0)
    g1 = cores(1, 0, 2, g1)
    next(rings)
    for k in (2, 3):
        to_right[k].wait_recv()
        to_left[k].wait_recv()
    g2 = spread(2, 0, 2)
    next(rings)
    g2 = cores(2, 0, 2, g2)
    next(rings)
    unpack(gathered_c, 1)
    lows[2] = dot(down_right_n[...], acts[1]).astype(bf16)
    def select(shape, test):
        row, column = (lax.broadcasted_iota(jnp.int32, shape, axis) for axis in (0, 1))
        return jnp.where(test(row, column), 1.0, 0.0).astype(bf16)

    def over_draws(ref):
        total = (ref[0].astype(f32) + ref[1].astype(f32)) + (ref[2].astype(f32) + ref[3].astype(f32))
        return (scale_grad * total).astype(bf16)

    def sum_units(out, box):
        total = out[tensor].astype(f32)
        for o in range(NT - 1):
            total = total + box[o].astype(f32)
        return total

    z_order = (1, 7, 2, 6, 3, 5, 4)

    def spread_adapters(ref):
        mine = ref.at[tensor]
        near = [send(mine, mine, {"tensor": yl * NZ + ring(z + o, NZ)}) for o in z_order]
        return near, [send(mine, mine, y_lo)]

    def forward_adapters(ref, near, far, these):
        for at in these:
            near[at].wait_recv()
            there = ref.at[yl * NZ + ring(z - z_order[at], NZ)]
            far.append(send(there, there, y_lo))

    def down_ranks():
        chosen = select(
            (16 * NT, RANK),
            lambda row, column: jnp.logical_and((row & 15) < 4, column == (row >> 4) * 4 + (row & 15)),
        )
        boxed = dot(chosen, ranks[2 * RANK :, :]).astype(bf16)
        for unit in range(NT):
            down_rank_out[unit] = boxed[16 * unit : 16 * (unit + 1)]
        return [
            send(down_rank_out.at[peer], down_rank_in.at[o], {"tensor": peer})
            for o, peer in enumerate(tensor_peers)
        ]

    def down_draws(copies):
        for copy in copies:
            copy.wait_recv()
        total = sum_units(down_rank_out, down_rank_in).astype(bf16)
        rows_f = dot_nt(total, acts[1]).astype(bf16)
        third, folded = FEAT // 3, None
        for q in range(3):
            chosen = select(
                (16, 16),
                lambda row, column: jnp.logical_and(row == column + 4 * q, column < 4),
            )
            piece = dot(chosen, rows_f[:, q * third : (q + 1) * third])
            folded = piece if folded is None else folded + piece
        down_draw_in[x] = folded.astype(bf16)
        mine = down_draw_in.at[x]
        return [send(mine, mine, where) for where in x_peers]

    def down_spread(copies):
        for copy in copies:
            copy.wait_recv()
        down_adapters[tensor] = over_draws(down_draw_in)
        return spread_adapters(down_adapters)

    low_sum = send(lows, lows_core, to_core)
    d0 = spread(0, 2, 3)
    g0 = bend(0, g0)
    low_sum.wait_recv()
    lows_y_out[...] = (lows[...].astype(f32) + lows_core[...].astype(f32)).astype(bf16)
    low_sum = send(lows_y_out, lows_y_in, y_hi)
    d0 = cores(0, 2, 3, d0)
    for copy in last[:4]:
        copy.wait_recv()
    g3 = spread(3, 0, 2)
    flip_back(0, 2, 0, 6)
    g3 = cores(3, 0, 2, g3)
    g1 = bend(1, g1)
    finish(g0)
    low_sum.wait_recv()
    lows_all[...] = (lows_y_out[...].astype(f32) + lows_y_in[...].astype(f32)).astype(bf16)
    for copy in last[4:8]:
        copy.wait_recv()
    g4 = spread(4, 0, 2)
    finish(g1)
    g4 = cores(4, 0, 2, g4)
    flip_back(0, 2, 6, 9)
    g2 = bend(2, g2)
    to_right[4].wait_recv()
    to_left[4].wait_recv()
    forward(2, 0, 80)
    forward(2, 80, 64)
    d1 = spread(1, 2, 3)
    d0 = bend_grad(0, d0)
    finish(g2)
    d1 = cores(1, 2, 3, d1)
    g3 = bend(3, g3)
    finish(d0)
    finish(g3)
    to_right[5].wait_recv()
    to_left[5].wait_recv()
    d2 = spread(2, 2, 3)
    g4 = bend(4, g4)
    d2 = cores(2, 2, 3, d2)
    flip_back(2, 3, 0, 6)
    lax.fori_loop(0, 4, early_outputs, 0)
    finish(g4)
    for copy in last[8:10]:
        copy.wait_recv()
    d3 = spread(3, 2, 3)
    d1 = bend_grad(1, d1)
    d3 = cores(3, 2, 3, d3)
    for copy in last[10:]:
        copy.wait_recv()
    d4 = spread(4, 2, 3)
    ranks[pl.ds(2 * RANK, RANK), :] = dot(right_a[2], all_tokens(2)).astype(bf16)
    flip_back(2, 3, 6, 9)
    d4 = cores(4, 2, 3, d4)
    down_sums = down_ranks()

    def outputs(half, group):
        m = half * 2 + group
        at = pl.ds(pl.multiple_of(m * SHARD, 16), SHARD)
        out = early_out[at, :] + dot(noisy_t[2, at, EARLY:], all_tokens(2, EARLY))
        out = out + dot(left_c[2, at, :], ranks[128:192, :])
        for i in range(4):
            pieces[4 * m + i] = side_by_side(out[i * OWN : (i + 1) * OWN]).astype(bf16)
        return group

    def pass_on(step, half, up, copy):
        target = half * NZ + (ring(z + 4 - step, NZ) if up else ring(z - 4 + step, NZ))
        box = (up_in if up else down_in).at[step, half]
        if copy is not None:
            copy.wait_recv()
            came = (up_in if up else down_in)[step - 1, half]
            pieces[target] = (pieces[target].astype(f32) + came.astype(f32)).astype(bf16)
        return send(pieces.at[target], box, z_up if up else z_down)

    flight = {}

    def go(step, half, up):
        flight[half, up] = pass_on(step, half, up, flight.get((half, up)))

    lax.fori_loop(0, 2, outputs, 1 - z // 4)
    go(0, 0, True)
    go(0, 1, False)
    lax.fori_loop(0, 2, outputs, z // 4)
    go(1, 1, True)
    go(1, 0, False)
    d2 = bend_grad(2, d2)
    finish(d1)
    finish(d2)
    d3 = bend_grad(3, d3)
    lax.fori_loop(0, 4, early_grads, 0)
    d4 = bend_grad(4, d4)
    go(1, 0, True)
    go(1, 1, False)
    finish(d3)
    finish(d4)

    for k in (0, 1):
        ranks[pl.ds(k * RANK, RANK), :] = dot(right_a[k], all_tokens(k)).astype(bf16)
    halves = []
    for half in (0, 1):
        chosen = select(
            (8 * NT, 2 * RANK),
            lambda row, column: column == ((row & 7) >> 2) * RANK + (row >> 3) * 4 + (row & 3),
        )
        halves.append(dot(chosen, ranks[: 2 * RANK, half * HALFT : (half + 1) * HALFT]))
    for unit in range(NT):
        at = slice(8 * unit, 8 * (unit + 1))
        rank_out[unit] = jnp.concatenate([halves[0][at], halves[1][at]]).astype(bf16)
    r1 = [
        send(rank_out.at[peer], rank_in.at[o], {"tensor": peer})
        for o, peer in enumerate(tensor_peers)
    ]

    quarter = core * 2 + yh
    for piece, (first, size) in enumerate(PARTS):
        at = place(quarter, piece)
        turned = [
            dot_nt(
                jnp.concatenate([back[b % 2, b // 2, k, at, :] for b in range(4)], axis=1),
                lows_all[k],
            )
            for k in (0, 1, 2, 2)
        ]
        hid_draw[x, pl.ds(first, size), :] = jnp.concatenate(turned, axis=1).astype(bf16)
    h3 = [send(hid_draw.at[x], hid_draw.at[x], where) for where in x_peers]
    own_rows = pl.ds(pl.multiple_of(quarter * SHARD, 16), SHARD)
    far_rows = pl.ds(pl.multiple_of((core * 2 + 1 - yh) * SHARD, 16), SHARD)

    def grads(half, group):
        m = half * 2 + group
        at = pl.ds(pl.multiple_of(m * SHARD, 16), SHARD)
        grad = early_grad[at, :] + dot(noisy_t[0, at, EARLY:], all_tokens(0, EARLY))
        grad = grad + dot(noisy_t[1, at, EARLY:], all_tokens(1, EARLY))
        grad = grad + dot(left_c[0, at, :], ranks[0:64, :]) + dot(left_c[1, at, :], ranks[64:128, :])
        for i in range(4):
            y_pieces[4 * m + i] = side_by_side(grad[i * OWN : (i + 1) * OWN]).astype(bf16)
        return group

    def cross_y(target):
        at = (1 - yl) * NZ + ring(target, NZ)
        return send(y_pieces.at[at], y_pieces_in.at[ring(target, NZ)], y_lo)

    def y_pass(step, up, copy, arrived):
        target = ring(z + 4 - step, NZ) if up else ring(z - 3 + step, NZ)
        box = y_up_in if up else y_down_in
        arrived.wait_recv()
        total = y_pieces[yl * NZ + target].astype(f32) + y_pieces_in[target].astype(f32)
        if copy is not None:
            copy.wait_recv()
            total = total + box[step - 1].astype(f32)
        y_pieces[yl * NZ + target] = total.astype(bf16)
        return send(y_pieces.at[yl * NZ + target], box.at[step], z_up if up else z_down)

    lax.fori_loop(0, 2, grads, 1 - z // 4)
    crossed = {4: cross_y(z + 4)}
    go(2, 1, True)
    go(2, 0, False)
    down_sums = down_draws(down_sums)
    lax.fori_loop(0, 2, grads, z // 4)
    for away in (3, -3, 2, -2, 1, -1, 0):
        crossed[away] = cross_y(z + away)
    go(2, 0, True)
    go(2, 1, False)
    for copy in r1:
        copy.wait_recv()
    total = sum_units(rank_out, rank_in)
    total = jnp.concatenate([total[:8], total[8:]], axis=1).astype(bf16)
    total = jnp.concatenate([total.astype(f32)] * 2).astype(bf16)
    rows_f = dot_nt(total, acts[0])
    rest = jnp.concatenate([rows_f[8:, WIDE:], rows_f[8:, : 2 * WIDE - FEAT]], axis=1)
    draw_in[x] = jnp.concatenate([rows_f[:8, :WIDE], rest]).astype(bf16)
    d1 = [send(draw_in.at[x], draw_in.at[x], where) for where in x_peers]
    down_near, down_far = down_spread(down_sums)
    y_up = y_pass(0, True, None, crossed[4])
    go(3, 1, True)
    go(3, 0, False)
    y_down = y_pass(0, False, None, crossed[-3])
    go(3, 0, True)
    go(3, 1, False)
    for copy in d1:
        copy.wait_recv()
    adapters[tensor] = over_draws(draw_in)
    near, far = spread_adapters(adapters)
    forward_adapters(down_adapters, down_near, down_far, range(7))
    y_up = y_pass(1, True, y_up, crossed[3])
    y_down = y_pass(1, False, y_down, crossed[-2])

    for copy in h3:
        copy.wait_recv()
    hid_all[own_rows, :] = over_draws(hid_draw)
    h4 = [
        send(hid_all.at[own_rows], hid_all.at[own_rows], y_hi),
        send(hid_all.at[own_rows], hid_all.at[own_rows], to_core),
    ]

    for copy in flight.values():
        copy.wait_recv()

    def over_z(half):
        return (
            pieces[half * NZ + z].astype(f32)
            + up_in[3, half].astype(f32)
            + down_in[3, half].astype(f32)
        )

    y_piece = (1 - yl) * NZ + z
    pieces[y_piece] = over_z(1 - yl).astype(bf16)
    cross = send(pieces.at[y_piece], cross_in, y_lo)
    y_up = y_pass(2, True, y_up, crossed[2])
    y_down = y_pass(2, False, y_down, crossed[-1])
    y_up = y_pass(3, True, y_up, crossed[1])

    forward_adapters(adapters, near, far, range(4))
    h4[0].wait_recv()
    h4.append(send(hid_all.at[far_rows], hid_all.at[far_rows], to_core))
    cross.wait_recv()
    first = over_z(yl) + cross_in[...].astype(f32)
    out_ref[:, :HALFT] = first[:OWN].astype(bf16)
    out_ref[:, HALFT:] = first[OWN:].astype(bf16)
    forward_adapters(adapters, near, far, range(4, 7))
    y_up.wait_recv()
    y_down.wait_recv()
    crossed[0].wait_recv()
    second = (
        (y_pieces[yl * NZ + z].astype(f32) + y_pieces_in[z].astype(f32))
        + y_up_in[3].astype(f32)
        + y_down_in[2].astype(f32)
    )
    grad_ref[:, :HALFT] = second[:OWN].astype(bf16)
    grad_ref[:, HALFT:] = second[OWN:].astype(bf16)
    h4[1].wait_recv()
    h4[2].wait_recv()
    turned = hid_all[...].astype(f32).T
    right_ref[0] = turned[:RANK].astype(bf16)
    right_ref[1] = turned[RANK : 2 * RANK].astype(bf16)
    down_left_ref[...] = turned[2 * RANK : 3 * RANK].astype(bf16)
    for copy in down_far:
        copy.wait_recv()
    stacked = jnp.concatenate([down_adapters[unit] for unit in range(NT)])
    for q in range(3):
        chosen = select(
            (RANK, 16 * NT), lambda row, column: column == (row >> 2) * 16 + (row & 3) + 4 * q
        )
        third = slice(q * FEAT // 3, (q + 1) * FEAT // 3)
        down_right_ref[:, third] = dot(chosen, stacked).astype(bf16)
    for copy in far:
        copy.wait_recv()
    stacked = jnp.concatenate([adapters[unit] for unit in range(NT)])
    for q in (0, 1):
        chosen = select(
            (2 * RANK, 16 * NT),
            lambda row, column: column
            == ((row & 63) >> 2) * 16 + (row >> 6) * 4 + (row & 3) + 8 * q,
        )
        wide = WIDE if q == 0 else FEAT - WIDE
        turned = dot(chosen, stacked[:, :wide]).astype(bf16)
        at = slice(q * WIDE, q * WIDE + wide)
        left_ref[0, :, at] = turned[:RANK]
        left_ref[1, :, at] = turned[RANK:]
    for copy in started:
        copy.wait_send()


def hand_over(*refs):
    for source, target in zip(refs[:6], refs[6:]):
        target[...] = source[...]


def on_device(
    tokens,
    cotangent,
    gate_up_weight,
    down_weight,
    gate_up_noise,
    down_noise,
    gate_up_left,
    gate_up_right,
    down_left,
    down_right,
):
    scale_grad = (NX * TOK) ** (-0.5)
    vmem, anywhere = pl.BlockSpec(memory_space=pltpu.VMEM), pl.BlockSpec(memory_space=pl.ANY)
    scratch = [
        pltpu.VMEM((3, HID, FEAT), bf16),
        pltpu.VMEM((3, HID, FEAT), bf16),
        pltpu.VMEM((3, FEAT, HID), bf16),
        pltpu.VMEM((NT, 2 * OWN, HALFT), bf16),
        pltpu.VMEM((NT, 2 * OWN, HALFT), bf16),
        pltpu.VMEM((2, FEAT, TOK), bf16),
        pltpu.VMEM((3, FEAT, RANK), bf16),
        pltpu.VMEM((3, HID, RANK), bf16),
        pltpu.VMEM((3, RANK, HID), bf16),
        pltpu.VMEM((3, RANK, TOK), bf16),
        pltpu.VMEM((3 * RANK, TOK), bf16),
        pltpu.VMEM((2, 2, 3, HID, LANES), bf16),
        pltpu.VMEM((2, 3, HID, LANES), bf16),
        pltpu.VMEM((2, 3, HID, LANES), bf16),
        pltpu.VMEM((2, 3, HID, LANES), bf16),
        pltpu.VMEM((2, 2, 3, HID, LANES), bf16),
        pltpu.VMEM((FEAT, TOK), f32),
        pltpu.VMEM((FEAT, TOK), f32),
        pltpu.VMEM((NT, 2 * OWN, HALFT), bf16),
        pltpu.VMEM((4, 2, 2 * OWN, HALFT), bf16),
        pltpu.VMEM((4, 2, 2 * OWN, HALFT), bf16),
        pltpu.VMEM((2 * OWN, HALFT), bf16),
        pltpu.VMEM((NT, 2 * OWN, HALFT), bf16),
        pltpu.VMEM((NZ, 2 * OWN, HALFT), bf16),
        pltpu.VMEM((4, 2 * OWN, HALFT), bf16),
        pltpu.VMEM((3, 2 * OWN, HALFT), bf16),
        pltpu.VMEM((NT, 16, HALFT), bf16),
        pltpu.VMEM((NT, 16, HALFT), bf16),
        pltpu.VMEM((NX, 16, WIDE), bf16),
        pltpu.VMEM((NT, 16, WIDE), bf16),
        pltpu.VMEM((NT, 16, TOK), bf16),
        pltpu.VMEM((NT, 16, TOK), bf16),
        pltpu.VMEM((NX, 16, FEAT // 3), bf16),
        pltpu.VMEM((NT, 16, FEAT // 3), bf16),
        pltpu.VMEM((3, RANK, TOK), bf16),
        pltpu.VMEM((3, RANK, TOK), bf16),
        pltpu.VMEM((3, RANK, TOK), bf16),
        pltpu.VMEM((3, RANK, TOK), bf16),
        pltpu.VMEM((NX, SHARD, 4 * RANK), bf16),
        pltpu.VMEM((HID, 4 * RANK), bf16),
        pltpu.SemaphoreType.DMA((MESSAGES,)),
        pltpu.SemaphoreType.DMA((MESSAGES,)),
        pltpu.SemaphoreType.DMA((16,)),
    ]
    shapes = [
        (OWN, TOK),
        (OWN, TOK),
        (2, RANK, FEAT),
        (2, RANK, HID),
        (RANK, HID),
        (RANK, FEAT),
    ]
    shapes = tuple(jax.ShapeDtypeStruct(shape, bf16) for shape in shapes)
    results = pl.pallas_call(
        functools.partial(kernel, scale_grad),
        out_shape=shapes,
        in_specs=[vmem] * 2 + [anywhere] * 4 + [vmem] * 4,
        out_specs=(vmem,) * 6,
        scratch_shapes=scratch,
        compiler_params=pltpu.CompilerParams(
            collective_id=0, has_side_effects=True, vmem_limit_bytes=62 * 2**20
        ),
    )(
        tokens[0].T,
        cotangent[0].T,
        jnp.swapaxes(gate_up_weight, 1, 2),
        down_weight,
        gate_up_noise[0],
        down_noise[0],
        jnp.swapaxes(gate_up_left, 1, 2),
        gate_up_right,
        down_left.T,
        down_right,
    )
    out, grad, left, right, down_left_grad, down_right_grad = pl.pallas_call(
        hand_over, out_shape=shapes, in_specs=[vmem] * 6, out_specs=(vmem,) * 6
    )(*results)
    return (
        out.T[None],
        grad.T[None],
        jnp.swapaxes(left, 1, 2),
        right,
        down_left_grad.T,
        down_right_grad,
    )


def solution(mesh):
    in_specs = (
        P("draw", None, ("batch", "tensor")),
        P("draw", None, ("batch", "tensor")),
        P(None, "batch", ("tensor", "draw")),
        P(("tensor", "draw"), "batch"),
        P("draw", None, "batch", "tensor"),
        P("draw", "tensor", "batch"),
        P(None, "batch", None),
        P(None, None, "tensor"),
        P("tensor", None),
        P(None, "batch"),
    )
    out_specs = (
        P("draw", None, ("batch", "tensor")),
        P("draw", None, ("batch", "tensor")),
        P(None, "batch", None),
        P(None, None, "tensor"),
        P("tensor", None),
        P(None, "batch"),
    )
    return jax.shard_map(
        on_device, mesh=mesh, in_specs=in_specs, out_specs=out_specs, check_vma=False
    )
```
